32 devices in a mesh: blk: 4 (over x, core), dom: 8 (over z, y).
Axes of the slice: x: 2, y: 2, z: 4, core: 2. Of those that a mesh axis runs over, the one named last changes fastest.
Arguments:
- nodes: bfloat16 [4096, 512], P(('blk', 'dom')), may hold values from -6 to 6
- experts_list: int32 [32, 1], P(('blk', 'dom')), may hold values from 0 to 3
- w_query: bfloat16 [512, 512], replicated
- w_key: bfloat16 [512, 512], replicated
- w_value: bfloat16 [512, 512], replicated, may hold values from -0.25 to 0.25
- w_out: bfloat16 [512, 512], replicated, may hold values from -0.25 to 0.25
- w_up: bfloat16 [512, 1024], replicated, may hold values from -0.25 to 0.25
- w_down: bfloat16 [1024, 512], replicated, may hold values from -0.1875 to 0.1875
- cotangent: bfloat16 [4096, 512], P(('blk', 'dom')), may hold values from -6 to 6
Outputs:
- layer_out: bfloat16 [4096, 512], P(('blk', 'dom'))
- grad_nodes: bfloat16 [4096, 512], P(('blk', 'dom'))
The draws below stay inside these ranges and needn't reach their ends.
Inputs may be any that keep to these rules, and one draw needn't show every extreme that they name: `experts_list`: row g names 1 different values; value c stands for the block held at blk index c and the same dom index as block g. Every value is named by some row.
All inputs are finite; a program needn't handle non-finite values.
Results may differ from the reference program's by a relative error of at most 0.0057.
Values may be sent and summed in bfloat16 or wider, within the bound.
No kernel may reach another device: no remote copies, remote signals or barrier semaphores. Data moves between devices by JAX's collectives and lax.ppermute only.
A program may use at most 128 MiB of HBM per device.

```python
import jax
import jax.numpy as jnp
from jax import lax

D = 512
H = 8
HEAD = 64
FF = 1024
BLOCK = 128
EXP = 1
NODES = 4096
N_BLK = 4
N_DOM = 8
DEVICES = 32


def projection_pair(key):
    first = jax.random.normal(jax.random.fold_in(key, 11), (D, D), jnp.float32) * D ** (-0.5)
    second = jax.random.normal(jax.random.fold_in(key, 12), (D, D), jnp.float32) * D ** (-0.5)
    return (first, second)


def draw_w_query(key, part):
    first, second = projection_pair(key)
    return first.astype(jnp.bfloat16)


def draw_w_key(key, part):
    first, second = projection_pair(key)
    result = second
    return result.astype(jnp.bfloat16)


def steps_of(stream_key, shape, split, smallest, high):
    def one(position, parts):
        heights = jax.random.uniform(jax.random.fold_in(jax.random.fold_in(stream_key, 6), position), (parts,), jnp.float32, smallest / len(split), high / len(split))
        return jnp.repeat(jnp.exp(heights), shape[position] // parts).reshape((-1,) + (1,) * (len(shape) - position - 1))

    gain = one(*split[0])
    for cut in split[1:]:
        gain = gain * one(*cut)
    return gain


def different_ones(stream_key, rows, count, top, lift):
    ranking = jax.random.permutation(jax.random.fold_in(stream_key, 1), count)
    pull = ranking
    for power in range(3):
        pull = pull * pull // count
    pull = pull * lift // count
    tickets = jax.random.randint(jax.random.fold_in(stream_key, 2), (rows, count), 0, 4096) + pull
    sure = jax.random.permutation(jax.random.fold_in(stream_key, 3), rows)[jnp.arange(count) % rows]
    tickets = jnp.where(jnp.arange(rows)[:, None] == sure[None, :], 1 << 14, tickets)
    merit = tickets * count + jnp.arange(count)
    return lax.top_k(merit.astype(jnp.int32), top)[1].astype(jnp.int32)


def centred(stream_key, dims, scale, limit, cuts=(), held_as=jnp.bfloat16):
    values = jax.random.normal(stream_key, dims, jnp.float32) * scale
    if len(cuts) > 0:
        values = steps_of(stream_key, dims, cuts, -0.22, 0.18) * values
    return jnp.clip(values, min=-limit, max=limit).astype(held_as)


def setup_inputs(seed: int = 0) -> dict:
    key_of = jax.random.split(jax.random.key(seed), 10)
    nodes = centred(key_of[0], (NODES, D), 1.0, 6.0, ((0, 32),))
    experts_list = different_ones(key_of[1], DEVICES, N_BLK, EXP, 4096)
    w_query = draw_w_query(jax.random.fold_in(key_of[9], 71), 0)
    w_key = draw_w_key(jax.random.fold_in(key_of[9], 71), 0)
    w_value = centred(key_of[4], (D, D), D ** -0.5, 0.25)
    w_out = centred(key_of[5], (D, D), D ** -0.5, 0.25)
    w_up = centred(key_of[6], (D, FF), D ** -0.5, 0.25)
    w_down = centred(key_of[7], (FF, D), FF ** -0.5, 0.1875)
    cotangent = centred(key_of[8], (NODES, D), 1.0, 6.0, ((0, 32),))
    return {"nodes": nodes, "experts_list": experts_list, "w_query": w_query, "w_key": w_key, "w_value": w_value, "w_out": w_out, "w_up": w_up, "w_down": w_down, "cotangent": cotangent}


EPS = 1e-05
NEG = -1e+30

def normalize(values):
    mean_v = lax.optimization_barrier(jnp.mean(values, axis=-1, keepdims=True))
    centered = values - mean_v
    inv_std = lax.rsqrt(lax.optimization_barrier(jnp.mean(centered * centered, axis=-1, keepdims=True)) + EPS)
    return (centered * inv_std, inv_std)

def normalize_back(values, upstream):
    unit, inv_std = normalize(values)
    return inv_std * (upstream - lax.optimization_barrier(jnp.mean(upstream, axis=-1, keepdims=True)) - unit * lax.optimization_barrier(jnp.mean(upstream * unit, axis=-1, keepdims=True)))

def heads_of(rows):
    return rows.reshape(rows.shape[0], H, HEAD).astype(jnp.float32)

def rounded(values):
    return lax.optimization_barrier(values.astype(jnp.bfloat16)).astype(jnp.float32)

def attend(queries, keyvals):
    qh = heads_of(queries)
    kh = heads_of(keyvals[:, :D])
    vh = heads_of(keyvals[:, D:])
    scores = jnp.einsum('qhd,khd->hqk', qh, kh) * HEAD ** (-0.5)
    top = lax.optimization_barrier(jnp.max(scores, axis=-1, keepdims=True))
    weights = jnp.exp(scores - top)
    total = lax.optimization_barrier(jnp.sum(weights, axis=-1, keepdims=True))
    mixed = jnp.einsum('hqk,khd->qhd', rounded(weights), vh)
    mixed = mixed / jnp.transpose(total, (1, 0, 2))
    lse = (top + jnp.log(total))[..., 0]
    return (mixed.reshape(queries.shape[0], D).astype(jnp.bfloat16), lse)

def attend_back(queries, keyvals, grad_out, lse, delta):
    qh = heads_of(queries)
    kh = heads_of(keyvals[:, :D])
    vh = heads_of(keyvals[:, D:])
    gh = heads_of(grad_out)
    scores = jnp.einsum('qhd,khd->hqk', qh, kh) * HEAD ** (-0.5)
    probs = jnp.exp(scores - lse[..., None])
    grad_v = jnp.einsum('hqk,qhd->khd', rounded(probs), gh)
    dprob = jnp.einsum('qhd,khd->hqk', gh, vh)
    dscore = rounded(probs * (dprob - delta[..., None]) * HEAD ** (-0.5))
    grad_q = jnp.einsum('hqk,khd->qhd', dscore, kh)
    grad_k = jnp.einsum('hqk,qhd->khd', dscore, qh)
    count = keyvals.shape[0]
    return (grad_q.reshape(queries.shape[0], D), jnp.concatenate([grad_k.reshape(count, D), grad_v.reshape(count, D)], 1))

def reference(nodes, experts_list, w_query, w_key, w_value, w_out, w_up, w_down, cotangent):
    f32 = jnp.float32
    bf16 = jnp.bfloat16
    x_full = nodes.astype(f32)
    unit, _ = normalize(x_full)
    normed = unit.astype(bf16)
    queries = jnp.dot(normed, w_query, preferred_element_type=f32).astype(bf16)
    keys = jnp.dot(normed, w_key, preferred_element_type=f32).astype(bf16)
    values = jnp.dot(normed, w_value, preferred_element_type=f32).astype(bf16)
    keyvals = jnp.concatenate([keys, values], 1).reshape(N_BLK, N_DOM, BLOCK, 2 * D)
    before = jnp.roll(keyvals, 1, axis=1)
    after = jnp.roll(keyvals, -1, axis=1)
    qblocks = queries.reshape(DEVICES, BLOCK, D)

    def gather_keys(index):
        brow = index // N_DOM
        dcol = index % N_DOM
        local = jnp.concatenate([before[brow, dcol], keyvals[brow, dcol], after[brow, dcol]], 0)
        far = keyvals[experts_list[index], dcol].reshape(EXP * BLOCK, 2 * D)
        return jnp.concatenate([local, far], 0)

    def forward_block(index):
        return attend(qblocks[index], gather_keys(index))
    order = jnp.arange(DEVICES, dtype=jnp.int32)
    mixed, lse = lax.map(forward_block, order)
    mixed_rows = mixed.reshape(NODES, D)
    resid = x_full + jnp.dot(mixed_rows, w_out, preferred_element_type=f32)
    unit2, _ = normalize(resid)
    normed2 = unit2.astype(bf16)
    pre = jnp.dot(normed2, w_up, preferred_element_type=f32)
    act, gelu_back = jax.vjp(jax.nn.gelu, pre)
    layer_out = (resid + jnp.dot(act.astype(bf16), w_down, preferred_element_type=f32)).astype(bf16)
    grad_act = jnp.dot(cotangent, w_down.T, preferred_element_type=f32)
    grad_pre = gelu_back(grad_act)[0].astype(bf16)
    grad_norm2 = jnp.dot(grad_pre, w_up.T, preferred_element_type=f32)
    grad_resid = cotangent.astype(f32) + normalize_back(resid, grad_norm2)
    grad_mixed = jnp.dot(grad_resid.astype(bf16), w_out.T, preferred_element_type=f32).astype(bf16)
    gblocks = grad_mixed.reshape(DEVICES, BLOCK, D)
    delta = lax.optimization_barrier(jnp.sum(grad_mixed.reshape(DEVICES, BLOCK, H, HEAD).astype(f32) * mixed.reshape(DEVICES, BLOCK, H, HEAD).astype(f32), axis=-1))
    delta = jnp.transpose(delta, (0, 2, 1))

    def back_step(sums, index):
        brow = index // N_DOM
        dcol = index % N_DOM
        grad_q, grad_kv = attend_back(qblocks[index], gather_keys(index), gblocks[index], lse[index], delta[index])
        sums = sums.at[brow, (dcol - 1) % N_DOM].add(grad_kv[:BLOCK])
        sums = sums.at[brow, dcol].add(grad_kv[BLOCK:2 * BLOCK])
        sums = sums.at[brow, (dcol + 1) % N_DOM].add(grad_kv[2 * BLOCK:3 * BLOCK])
        sums = sums.at[experts_list[index], dcol].add(grad_kv[3 * BLOCK:].reshape(EXP, BLOCK, 2 * D))
        return (sums, grad_q)
    sums, grad_q_all = lax.scan(back_step, jnp.zeros((N_BLK, N_DOM, BLOCK, 2 * D), f32), order)
    grad_kv = sums.reshape(NODES, 2 * D)
    grad_in = jnp.dot(grad_q_all.reshape(NODES, D).astype(bf16), w_query.T, preferred_element_type=f32) + jnp.dot(grad_kv[:, :D].astype(bf16), w_key.T, preferred_element_type=f32) + jnp.dot(grad_kv[:, D:].astype(bf16), w_value.T, preferred_element_type=f32)
    grad_nodes = (grad_resid + normalize_back(x_full, grad_in)).astype(bf16)
    return (layer_out, grad_nodes)
```

```python
import functools

import jax
import jax.numpy as jnp
from jax import lax
from jax.experimental import pallas as pl
from jax.experimental.pallas import tpu as pltpu
from jax.sharding import PartitionSpec as P

H = 8
HEAD = 64
EPS = 1e-05
SCALE = HEAD ** (-0.5)
PAIR = 2 * HEAD
GELU_C = 0.7978845608028654
GELU_A = 0.044715
MIB = 1 << 20

f32 = jnp.float32
bf16 = jnp.bfloat16


def dot(a, b):
    return jnp.dot(a, b, preferred_element_type=f32)


def dot_t(a, b):
    return lax.dot_general(a, b, (((1,), (1,)), ((), ())), preferred_element_type=f32)


def t_dot(a, b):
    return lax.dot_general(a, b, (((0,), (0,)), ((), ())), preferred_element_type=f32)


def normalize(values):
    mean_v = jnp.mean(values, axis=-1, keepdims=True)
    centered = values - mean_v
    inv_std = lax.rsqrt(jnp.mean(centered * centered, axis=-1, keepdims=True) + EPS)
    return (centered * inv_std, inv_std)


def normalize_back(unit, inv_std, upstream):
    return inv_std * (
        upstream
        - jnp.mean(upstream, axis=-1, keepdims=True)
        - unit * jnp.mean(upstream * unit, axis=-1, keepdims=True)
    )


def halves(rows):
    left = lax.broadcasted_iota(jnp.int32, rows.shape, 1) < HEAD
    zero = jnp.zeros_like(rows)
    return jnp.concatenate([jnp.where(left, rows, zero), jnp.where(left, zero, rows)], 0)


def unhalve(both):
    n = both.shape[1] // 2
    first, second = both[:, :n], both[:, n:]
    upper = lax.broadcasted_iota(jnp.int32, first.shape, 0) < HEAD
    return jnp.where(upper, first, second).T


def own_kernel(x_ref, cot_ref, wq_ref, wk_ref, wv_ref, wdown_ref, q_ref, k_ref, v_ref, gact_ref):
    unit, _ = normalize(x_ref[...].astype(f32))
    normed = unit.astype(bf16)
    q_ref[...] = (dot(normed, wq_ref[...]) * SCALE).astype(bf16)
    k_ref[...] = dot(normed, wk_ref[...]).astype(bf16)
    v_ref[...] = dot(normed, wv_ref[...]).astype(bf16)
    gact_ref[...] = dot_t(cot_ref[...], wdown_ref[...])


def main_kernel(groups, listed, *refs):
    experts_ref, place_ref = refs[:2]
    slots = refs[2 : 2 + groups]
    (near_a, near_b, q_ref, k_ref, v_ref, gact_ref, cot_ref, wk_ref, wv_ref, wout_ref, wup_ref) = refs[
        2 + groups : 13 + groups
    ]
    outs = refs[13 + groups :]
    far_count = groups.bit_length() - 1
    send_a, send_b, keep = outs[:3]
    sends = outs[3 : 3 + far_count]
    gq_ref, gkv_ref, act_ref, resid_ref, gres_ref = outs[3 + far_count : 8 + far_count]
    chosen_s, k_s, v_s, w_s, inv_s, mixed_s, gk_s, gv_s = outs[8 + far_count :]
    x_ref = slots[0]
    rows, width = x_ref.shape
    picked = [experts_ref[0, e] ^ place_ref[0] for e in range(listed)]
    for e in range(listed):
        for slot in range(groups):

            @pl.when(picked[e] == slot)
            def _(e=e, slot=slot):
                chosen_s[e * rows : (e + 1) * rows, :] = slots[slot][...]

    def project(block, at):
        unit, _ = normalize(block.astype(f32))
        normed = unit.astype(bf16)
        k_s[at : at + block.shape[0], :] = dot(normed, wk_ref[...]).astype(bf16)
        v_s[at : at + block.shape[0], :] = dot(normed, wv_ref[...]).astype(bf16)

    k_s[:rows, :] = k_ref[...]
    v_s[:rows, :] = v_ref[...]
    others = jnp.concatenate([near_a[...], near_b[...], chosen_s[...]], 0)
    project(others, rows)

    for j in range(H // 2):
        cols = slice(j * PAIR, (j + 1) * PAIR)
        q2 = halves(q_ref[:, cols])
        scores = dot_t(k_s[:, cols], q2)
        weights = jnp.exp(scores - jnp.max(scores, axis=0, keepdims=True))
        inv = 1.0 / jnp.sum(weights, axis=0, keepdims=True)
        w_s[j] = weights
        inv_s[j] = inv
        mixed = t_dot(v_s[:, cols], weights.astype(bf16)) * inv
        mixed_s[:, cols] = unhalve(mixed).astype(bf16)

    mixed = mixed_s[...]
    resid = x_ref[...].astype(f32) + dot(mixed, wout_ref[...])
    resid_ref[...] = resid
    unit2, inv2 = normalize(resid)
    pre = dot(unit2.astype(bf16), wup_ref[...])
    square = pre * pre
    tanh = jnp.tanh(GELU_C * pre * (1.0 + GELU_A * square))
    act_ref[...] = (0.5 * pre * (1.0 + tanh)).astype(bf16)
    slope = 0.5 * (1.0 + tanh) + (0.5 * GELU_C) * pre * (1.0 - tanh * tanh) * (
        1.0 + (3.0 * GELU_A) * square
    )
    gpre = (gact_ref[...] * slope).astype(bf16)
    gres = cot_ref[...].astype(f32) + normalize_back(unit2, inv2, dot_t(gpre, wup_ref[...]))
    gres_ref[...] = gres
    gmixed = dot_t(gres.astype(bf16), wout_ref[...]).astype(bf16)
    prod = gmixed.astype(f32) * mixed.astype(f32)
    high = prod.astype(bf16)
    low = (prod - high.astype(f32)).astype(bf16)
    head_of = lax.broadcasted_iota(jnp.int32, (H, width), 1) // HEAD
    ones = (head_of == lax.broadcasted_iota(jnp.int32, (H, width), 0)).astype(bf16)
    delta = dot_t(ones, high) + dot_t(ones, low)

    for j in range(H // 2):
        cols = slice(j * PAIR, (j + 1) * PAIR)
        q2 = halves(q_ref[:, cols])
        g2 = halves(gmixed[:, cols])
        row = jnp.concatenate([delta[2 * j : 2 * j + 1, :], delta[2 * j + 1 : 2 * j + 2, :]], 1)
        probs = w_s[j] * inv_s[j]
        ds = (probs * (dot_t(v_s[:, cols], g2) - row)).astype(bf16)
        gv_s[:, cols] = dot(probs.astype(bf16), g2).astype(bf16)
        gk_s[:, cols] = dot(ds, q2).astype(bf16)
        gq_ref[:, cols] = (unhalve(t_dot(k_s[:, cols], ds)) * SCALE).astype(bf16)

    gkv_ref[:, :width] = gk_s[:rows, :]
    gkv_ref[:, width:] = gv_s[:rows, :]
    parts = dot_t(gk_s[rows:, :], wk_ref[...]) + dot_t(gv_s[rows:, :], wv_ref[...])
    send_a[...] = parts[:rows].astype(bf16)
    send_b[...] = parts[rows : 2 * rows].astype(bf16)

    def far(slot):
        total = jnp.zeros((rows, width), f32)
        for e in range(listed):
            part = parts[(2 + e) * rows : (3 + e) * rows]
            total = total + jnp.where(picked[e] == slot, part, 0.0)
        return total

    keep[...] = far(0)
    for bit in range(far_count):
        for i in range(1 << bit):
            sends[bit][i * rows : (i + 1) * rows, :] = far((1 << bit) + i).astype(bf16)


def rest_kernel(gq_ref, gkv_ref, keep_ref, act_ref, resid_ref, wq_ref, wk_ref, wv_ref, wdown_ref, out_ref, acc_ref):
    width = gq_ref.shape[1]
    acc_ref[...] = (
        keep_ref[...]
        + dot_t(gq_ref[...], wq_ref[...])
        + dot_t(gkv_ref[:, :width], wk_ref[...])
        + dot_t(gkv_ref[:, width:], wv_ref[...])
    )
    out_ref[...] = (resid_ref[...] + dot(act_ref[...], wdown_ref[...])).astype(bf16)


def last_kernel(x_ref, gres_ref, acc_ref, *refs):
    out_ref = refs[-1]
    rows = x_ref.shape[0]
    total = acc_ref[...]
    for part in refs[:-1]:
        total = total + part[:rows, :].astype(f32)
    unit, inv = normalize(x_ref[...].astype(f32))
    out_ref[...] = (gres_ref[...] + normalize_back(unit, inv, total)).astype(bf16)


def call(kernel, outs, args, scratch=(), flops=0, smem=0):
    whole = pl.BlockSpec(memory_space=pltpu.VMEM)
    small = pl.BlockSpec(memory_space=pltpu.SMEM)
    return pl.pallas_call(
        kernel,
        out_shape=[jax.ShapeDtypeStruct(shape, dtype) for shape, dtype in outs],
        in_specs=[small] * smem + [whole] * (len(args) - smem),
        out_specs=[whole] * len(outs),
        scratch_shapes=list(scratch),
        compiler_params=pltpu.CompilerParams(vmem_limit_bytes=40 * MIB),
        cost_estimate=pl.CostEstimate(flops=flops, bytes_accessed=4 * MIB, transcendentals=0),
    )(*args)


def on_device(nodes, experts_list, w_query, w_key, w_value, w_out, w_up, w_down, cotangent):
    rows, width = nodes.shape
    hidden = w_up.shape[1]
    groups = lax.axis_size("blk")
    domains = lax.axis_size("dom")
    listed = experts_list.shape[1]
    bits = groups.bit_length() - 1
    place = lax.axis_index("blk").astype(jnp.int32).reshape(1)

    def across(array, bit):
        return lax.ppermute(array, "blk", [(i, i ^ (1 << bit)) for i in range(groups)])

    pairs_a = [(i, i ^ 1) for i in range(domains)]
    pairs_b = []
    for i in range(1, domains, 2):
        pairs_b += [(i, (i + 1) % domains), ((i + 1) % domains, i)]

    held = {0: nodes}
    top = bits - 1
    held[1 << top] = across(nodes, top)
    near_b = lax.ppermute(nodes, "dom", pairs_b)
    near_a = lax.ppermute(nodes, "dom", pairs_a)
    for bit in range(top - 1, -1, -1):
        for slot in list(held):
            held[slot | (1 << bit)] = across(held[slot], bit)

    q, k, v, gact = call(
        own_kernel,
        [((rows, width), bf16)] * 3 + [((rows, hidden), f32)],
        [nodes, cotangent, w_query, w_key, w_value, w_down],
        flops=2 * rows * width * (3 * width + hidden),
    )
    keys = (3 + listed) * rows
    outs = call(
        functools.partial(main_kernel, groups, listed),
        [((rows, width), bf16)] * 2
        + [((rows, width), f32)]
        + [(((1 << bit) * rows, width), bf16) for bit in range(bits)]
        + [((rows, width), bf16), ((rows, 2 * width), bf16), ((rows, hidden), bf16)]
        + [((rows, width), f32)] * 2,
        [experts_list, place]
        + [held[slot] for slot in range(groups)]
        + [near_a, near_b, q, k, v, gact, cotangent, w_key, w_value, w_out, w_up],
        [
            pltpu.VMEM((listed * rows, width), bf16),
            pltpu.VMEM((keys, width), bf16),
            pltpu.VMEM((keys, width), bf16),
            pltpu.VMEM((H // 2, keys, 2 * rows), f32),
            pltpu.VMEM((H // 2, 1, 2 * rows), f32),
            pltpu.VMEM((rows, width), bf16),
            pltpu.VMEM((keys, width), bf16),
            pltpu.VMEM((keys, width), bf16),
        ],
        flops=2 * rows * width * (8 * keys + 4 * hidden),
        smem=2,
    )
    send_a, send_b, keep = outs[:3]
    sends = list(outs[3 : 3 + bits])
    gq, gkv, act, resid, gres = outs[3 + bits :]

    received = []
    for bit in range(top, -1, -1):
        lo, hi = (1 << bit) * rows, (2 << bit) * rows
        part = sends[bit]
        if received:
            total = part.astype(f32)
            for earlier in received:
                total = total + earlier[lo:hi].astype(f32)
            part = total.astype(bf16)
        received.append(across(part, bit))
        if bit == top:
            from_b = lax.ppermute(send_b, "dom", pairs_b)
            from_a = lax.ppermute(send_a, "dom", pairs_a)

    layer_out, acc = call(
        rest_kernel,
        [((rows, width), bf16), ((rows, width), f32)],
        [gq, gkv, keep, act, resid, w_query, w_key, w_value, w_down],
        flops=2 * rows * width * (3 * width + hidden),
    )
    (grad_nodes,) = call(
        last_kernel,
        [((rows, width), bf16)],
        [nodes, gres, acc, from_a, from_b] + received,
    )
    return (layer_out, grad_nodes)


def solution(mesh):
    split = P(("blk", "dom"), None)
    return jax.shard_map(
        on_device,
        mesh=mesh,
        in_specs=(split, split, P(), P(), P(), P(), P(), P(), split),
        out_specs=(split, split),
        check_vma=False,
    )
```

```python
import functools

import jax
import jax.numpy as jnp
from jax import lax
from jax.experimental import pallas as pl
from jax.experimental.pallas import tpu as pltpu
from jax.sharding import PartitionSpec as P

H = 8
HEAD = 64
EPS = 1e-05
SCALE = HEAD ** (-0.5)
PAIR = 2 * HEAD
GELU_C = 0.7978845608028654
GELU_A = 0.044715
MIB = 1 << 20

f32 = jnp.float32
bf16 = jnp.bfloat16


def dot(a, b):
    return jnp.dot(a, b, preferred_element_type=f32)


def dot_t(a, b):
    return lax.dot_general(a, b, (((1,), (1,)), ((), ())), preferred_element_type=f32)


def t_dot(a, b):
    return lax.dot_general(a, b, (((0,), (0,)), ((), ())), preferred_element_type=f32)


def normalize(values):
    mean_v = jnp.mean(values, axis=-1, keepdims=True)
    centered = values - mean_v
    inv_std = lax.rsqrt(jnp.mean(centered * centered, axis=-1, keepdims=True) + EPS)
    return (centered * inv_std, inv_std)


def normalize_back(unit, inv_std, upstream):
    return inv_std * (
        upstream
        - jnp.mean(upstream, axis=-1, keepdims=True)
        - unit * jnp.mean(upstream * unit, axis=-1, keepdims=True)
    )


def halves(rows):
    left = lax.broadcasted_iota(jnp.int32, rows.shape, 1) < HEAD
    zero = jnp.zeros_like(rows)
    return jnp.concatenate([jnp.where(left, rows, zero), jnp.where(left, zero, rows)], 0)


def unhalve(both):
    n = both.shape[1] // 2
    first, second = both[:, :n], both[:, n:]
    upper = lax.broadcasted_iota(jnp.int32, first.shape, 0) < HEAD
    return jnp.where(upper, first, second).T


def sent_slots(groups):
    return [range(1 << bit, groups, 2 << bit) for bit in range(groups.bit_length() - 1)]


def own_kernel(*refs):
    count = 8
    given, held = refs[:count], refs[count : 2 * count]
    q_ref, k_ref, v_ref, gact_ref, unit_ref, inv_ref, sem = refs[2 * count :]
    copies = [pltpu.make_async_copy(given[i], held[i], sem.at[i]) for i in range(count)]
    for copy in copies:
        copy.start()
    x_ref, cot_ref, wdown_ref, wk_ref, wv_ref, wq_ref = held[:6]
    copies[0].wait()
    unit, inv = normalize(x_ref[...].astype(f32))
    unit_ref[...] = unit
    inv_ref[...] = inv
    normed = unit.astype(bf16)
    copies[1].wait()
    copies[2].wait()
    gact_ref[...] = dot_t(cot_ref[...], wdown_ref[...])
    copies[3].wait()
    k_ref[...] = dot(normed, wk_ref[...]).astype(bf16)
    copies[4].wait()
    v_ref[...] = dot(normed, wv_ref[...]).astype(bf16)
    copies[5].wait()
    q_ref[...] = (dot(normed, wq_ref[...]) * SCALE).astype(bf16)
    copies[6].wait()
    copies[7].wait()


def pair_columns():
    return [(j, slice(j * PAIR, (j + 1) * PAIR)) for j in range(H // 2)]


def early_kernel(near_a, q_ref, k_ref, v_ref, wk_ref, wv_ref, ke_ref, ve_ref, se_ref):
    rows = q_ref.shape[0]
    unit, _ = normalize(near_a[...].astype(f32))
    normed = unit.astype(bf16)
    ke_ref[:rows, :] = k_ref[...]
    ve_ref[:rows, :] = v_ref[...]
    ke_ref[rows:, :] = dot(normed, wk_ref[...]).astype(bf16)
    ve_ref[rows:, :] = dot(normed, wv_ref[...]).astype(bf16)
    for j, cols in pair_columns():
        se_ref[j] = dot_t(ke_ref[:, cols], halves(q_ref[:, cols]))


def block_back(v, q2, g2, weights, inv, row):
    probs = weights * inv
    ds = (probs * (dot_t(v, g2) - row)).astype(bf16)
    return ds, dot(ds, q2).astype(bf16), dot(probs.astype(bf16), g2).astype(bf16)


def delta_row(delta, j):
    return jnp.concatenate([delta[2 * j : 2 * j + 1, :], delta[2 * j + 1 : 2 * j + 2, :]], 1)


def main_kernel(groups, listed, *refs):
    experts_ref = refs[0]
    slots = refs[1 : 1 + groups]
    (near_b, x_ref, ke_ref, ve_ref, se_ref, q_ref, gact_ref, cot_ref) = refs[1 + groups : 9 + groups]
    (wk_ref, wv_ref, wout_ref, wup_ref) = refs[9 + groups : 13 + groups]
    outs = refs[13 + groups :]
    bits = groups.bit_length() - 1
    sends = outs[:bits]
    (keep, w_ref, inv_ref, gmixed_ref, delta_ref, kb_ref, vb_ref, ds_ref, act_ref, resid_ref, gres_ref) = outs[
        bits : bits + 11
    ]
    picked_s, mixed_s, gk_s, gv_s = outs[bits + 11 :]
    rows, width = x_ref.shape
    early = 2 * rows
    place = lax.axis_index("blk")
    picked = [experts_ref[0, e] ^ place for e in range(listed)]
    for e in range(listed):
        for i in range(groups):

            @pl.when(picked[e] == i)
            def _(e=e, i=i):
                picked_s[(1 + e) * rows : (2 + e) * rows, :] = slots[i][...]

    picked_s[:rows, :] = near_b[...]
    unit, _ = normalize(picked_s[...].astype(f32))
    normed = unit.astype(bf16)
    kb_ref[...] = dot(normed, wk_ref[...]).astype(bf16)
    vb_ref[...] = dot(normed, wv_ref[...]).astype(bf16)
    for j, cols in pair_columns():
        last = dot_t(kb_ref[:, cols], halves(q_ref[:, cols]))
        first = se_ref[j]
        top = jnp.maximum(jnp.max(first, axis=0, keepdims=True), jnp.max(last, axis=0, keepdims=True))
        first = jnp.exp(first - top)
        last = jnp.exp(last - top)
        inv = 1.0 / (jnp.sum(first, axis=0, keepdims=True) + jnp.sum(last, axis=0, keepdims=True))
        w_ref[j, :early, :] = first
        w_ref[j, early:, :] = last
        inv_ref[j] = inv
        mixed = t_dot(ve_ref[:, cols], first.astype(bf16)) + t_dot(vb_ref[:, cols], last.astype(bf16))
        mixed_s[:, cols] = unhalve(mixed * inv).astype(bf16)

    mixed = mixed_s[...]
    resid = x_ref[...].astype(f32) + dot(mixed, wout_ref[...])
    resid_ref[...] = resid
    unit2, inv2 = normalize(resid)
    pre = dot(unit2.astype(bf16), wup_ref[...])
    square = pre * pre
    tanh = jnp.tanh(GELU_C * pre * (1.0 + GELU_A * square))
    act_ref[...] = (0.5 * pre * (1.0 + tanh)).astype(bf16)
    slope = 0.5 * (1.0 + tanh) + (0.5 * GELU_C) * pre * (1.0 - tanh * tanh) * (
        1.0 + (3.0 * GELU_A) * square
    )
    gpre = (gact_ref[...] * slope).astype(bf16)
    gres = cot_ref[...].astype(f32) + normalize_back(unit2, inv2, dot_t(gpre, wup_ref[...]))
    gres_ref[...] = gres
    gmixed = dot_t(gres.astype(bf16), wout_ref[...]).astype(bf16)
    gmixed_ref[...] = gmixed
    prod = gmixed.astype(f32) * mixed.astype(f32)
    high = prod.astype(bf16)
    low = (prod - high.astype(f32)).astype(bf16)
    head_of = lax.broadcasted_iota(jnp.int32, (H, width), 1) // HEAD
    ones = (head_of == lax.broadcasted_iota(jnp.int32, (H, width), 0)).astype(bf16)
    delta = dot_t(ones, high) + dot_t(ones, low)
    delta_ref[...] = delta

    for j, cols in pair_columns():
        ds_ref[j], gk_s[:, cols], gv_s[:, cols] = block_back(
            vb_ref[rows:, cols],
            halves(q_ref[:, cols]),
            halves(gmixed[:, cols]),
            w_ref[j, early + rows :, :],
            inv_ref[j],
            delta_row(delta, j),
        )
    parts = dot_t(gk_s[...], wk_ref[...]) + dot_t(gv_s[...], wv_ref[...])

    def far(slot):
        total = jnp.zeros((rows, width), f32)
        for e in range(listed):
            total = total + jnp.where(picked[e] == slot, parts[e * rows : (e + 1) * rows], 0.0)
        return total

    keep[...] = far(0)
    for bit, slots_sent in enumerate(sent_slots(groups)):
        for i, slot in enumerate(slots_sent):
            sends[bit][i * rows : (i + 1) * rows, :] = far(slot).astype(bf16)


def near_kernel(
    w_ref, inv_ref, delta_ref, gmixed_ref, q_ref, ve_ref, vb_ref, wk_ref, wv_ref, send_a, send_b, ds_ref, gk_s, gv_s
):
    rows = send_a.shape[0]
    delta = delta_ref[...]
    for j, cols in pair_columns():
        ds_ref[j], gk_s[:, cols], gv_s[:, cols] = block_back(
            jnp.concatenate([ve_ref[rows:, cols], vb_ref[:rows, cols]], 0),
            halves(q_ref[:, cols]),
            halves(gmixed_ref[:, cols]),
            w_ref[j, rows : 3 * rows, :],
            inv_ref[j],
            delta_row(delta, j),
        )
    parts = dot_t(gk_s[...], wk_ref[...]) + dot_t(gv_s[...], wv_ref[...])
    send_a[...] = parts[:rows].astype(bf16)
    send_b[...] = parts[rows:].astype(bf16)


def rest_kernel(*refs):
    (w_ref, inv_ref, delta_ref, gmixed_ref, q_ref, ke_ref, ve_ref, kb_ref, far_ref, near_ref) = refs[:10]
    (keep_ref, act_ref, resid_ref, wq_ref, wk_ref, wv_ref, wdown_ref, out_ref, acc_ref) = refs[10:19]
    gq_s, gk_s, gv_s = refs[19:]
    rows = q_ref.shape[0]
    delta = delta_ref[...]
    for j, cols in pair_columns():
        ds, gk_s[:, cols], gv_s[:, cols] = block_back(
            ve_ref[:rows, cols],
            halves(q_ref[:, cols]),
            halves(gmixed_ref[:, cols]),
            w_ref[j, :rows, :],
            inv_ref[j],
            delta_row(delta, j),
        )
        total = t_dot(ke_ref[:rows, cols], ds) + t_dot(ke_ref[rows:, cols], near_ref[j, :rows])
        total = total + t_dot(kb_ref[:rows, cols], near_ref[j, rows:]) + t_dot(kb_ref[rows:, cols], far_ref[j])
        gq_s[:, cols] = (unhalve(total) * SCALE).astype(bf16)
    acc_ref[...] = (
        keep_ref[...] + dot_t(gq_s[...], wq_ref[...]) + dot_t(gk_s[...], wk_ref[...]) + dot_t(gv_s[...], wv_ref[...])
    )
    out_ref[...] = (resid_ref[...] + dot(act_ref[...], wdown_ref[...])).astype(bf16)


def last_kernel(unit_ref, inv_ref, gres_ref, acc_ref, *refs):
    out_ref = refs[-1]
    rows = unit_ref.shape[0]
    total = acc_ref[...]
    for part in refs[:-1]:
        total = total + part[:rows, :].astype(f32)
    out_ref[...] = (gres_ref[...] + normalize_back(unit_ref[...], inv_ref[...], total)).astype(bf16)


def call(kernel, outs, args, scratch=(), flops=0, smem=0, space=pltpu.VMEM):
    whole = pl.BlockSpec(memory_space=pltpu.VMEM)
    small = pl.BlockSpec(memory_space=pltpu.SMEM)
    return pl.pallas_call(
        kernel,
        out_shape=[jax.ShapeDtypeStruct(shape, dtype) for shape, dtype in outs],
        in_specs=[small] * smem + [pl.BlockSpec(memory_space=space)] * (len(args) - smem),
        out_specs=[whole] * len(outs),
        scratch_shapes=list(scratch),
        compiler_params=pltpu.CompilerParams(vmem_limit_bytes=40 * MIB),
        cost_estimate=pl.CostEstimate(flops=flops, bytes_accessed=4 * MIB, transcendentals=0),
    )(*args)


def on_device(nodes, experts_list, w_query, w_key, w_value, w_out, w_up, w_down, cotangent):
    rows, width = nodes.shape
    hidden = w_up.shape[1]
    groups = lax.axis_size("blk")
    domains = lax.axis_size("dom")
    listed = experts_list.shape[1]
    bits = groups.bit_length() - 1

    def across(array, bit):
        return lax.ppermute(array, "blk", [(i, i ^ (1 << bit)) for i in range(groups)])

    pairs_a = [(i, i ^ 1) for i in range(domains)]
    pairs_b = []
    for i in range(1, domains, 2):
        pairs_b += [(i, (i + 1) % domains), ((i + 1) % domains, i)]

    held = {0: nodes}
    top = bits - 1
    held[1 << top] = across(nodes, top)
    near_a = lax.ppermute(nodes, "dom", pairs_a)
    near_b = lax.ppermute(nodes, "dom", pairs_b)
    for bit in range(top - 1, -1, -1):
        for slot in list(held):
            held[slot | (1 << bit)] = across(held[slot], bit)

    given = [nodes, cotangent, w_down, w_key, w_value, w_query, w_out, w_up]
    *given, q, k, v, gact, unit, inv_std = call(
        own_kernel,
        [(array.shape, bf16) for array in given]
        + [((rows, width), bf16)] * 3
        + [((rows, hidden), f32), ((rows, width), f32), ((rows, 1), f32)],
        [pltpu.with_memory_space_constraint(array, pltpu.HBM) for array in given],
        [pltpu.SemaphoreType.DMA((len(given),))],
        flops=2 * rows * width * (3 * width + hidden),
        space=pltpu.HBM,
    )
    x, cotangent, w_down, w_key, w_value, w_query, w_out, w_up = given
    held[0] = x
    early = 2 * rows
    late = (1 + listed) * rows
    keys = early + late
    ke, ve, se = call(
        early_kernel,
        [((early, width), bf16)] * 2 + [((H // 2, early, 2 * rows), f32)],
        [near_a, q, k, v, w_key, w_value],
        flops=2 * early * width * (2 * width + 2 * rows),
    )
    sent = sent_slots(groups)
    outs = call(
        functools.partial(main_kernel, groups, listed),
        [((len(slots) * rows, width), bf16) for slots in sent]
        + [((rows, width), f32), ((H // 2, keys, 2 * rows), f32), ((H // 2, 1, 2 * rows), f32)]
        + [((rows, width), bf16), ((H, rows), f32), ((late, width), bf16), ((late, width), bf16)]
        + [((H // 2, listed * rows, 2 * rows), bf16), ((rows, hidden), bf16)]
        + [((rows, width), f32)] * 2,
        [experts_list] + [held[slot] for slot in range(groups)] + [near_b, x, ke, ve, se, q, gact, cotangent, w_key, w_value, w_out, w_up],
        [pltpu.VMEM((late, width), bf16), pltpu.VMEM((rows, width), bf16)]
        + [pltpu.VMEM((listed * rows, width), bf16)] * 2,
        flops=2 * rows * width * (6 * keys + 4 * hidden),
        smem=1,
    )
    sends = outs[:bits]
    keep, w, inv, gmixed, delta, kb, vb, ds_far, act, resid, gres = outs[bits:]
    received = [across(sends[0], 0)]
    send_a, send_b, ds_near = call(
        near_kernel,
        [((rows, width), bf16)] * 2 + [((H // 2, 2 * rows, 2 * rows), bf16)],
        [w, inv, delta, gmixed, q, ve, vb, w_key, w_value],
        [pltpu.VMEM((2 * rows, width), bf16)] * 2,
        flops=8 * rows * width * (width + 6 * rows),
    )
    from_b = lax.ppermute(send_b, "dom", pairs_b)
    from_a = lax.ppermute(send_a, "dom", pairs_a)
    for bit in range(1, bits):
        total = sends[bit].astype(f32)
        for lower, array in enumerate(received):
            blocks = array.reshape(-1, rows, width)[(1 << bit) >> (lower + 1) :: (2 << bit) >> (lower + 1)]
            total = total + blocks.reshape(-1, width).astype(f32)
        received.append(across(total.astype(bf16), bit))

    layer_out, acc = call(
        rest_kernel,
        [((rows, width), bf16), ((rows, width), f32)],
        [w, inv, delta, gmixed, q, ke, ve, kb, ds_far, ds_near, keep, act, resid, w_query, w_key, w_value, w_down],
        [pltpu.VMEM((rows, width), bf16)] * 3,
        flops=2 * rows * width * (3 * width + hidden + 8 * rows),
    )
    (grad_nodes,) = call(
        last_kernel,
        [((rows, width), bf16)],
        [unit, inv_std, gres, acc, from_a, from_b] + received,
    )
    return (layer_out, grad_nodes)


def solution(mesh):
    split = P(("blk", "dom"), None)
    return jax.shard_map(
        on_device,
        mesh=mesh,
        in_specs=(split, split, P(), P(), P(), P(), P(), P(), split),
        out_specs=(split, split),
        check_vma=False,
    )
```

```python
import functools

import jax
import jax.numpy as jnp
from jax import lax
from jax.experimental import pallas as pl
from jax.experimental.pallas import tpu as pltpu
from jax.sharding import PartitionSpec as P

H = 8
HEAD = 64
EPS = 1e-05
SCALE = HEAD ** (-0.5)
PAIR = 2 * HEAD
GELU_C = 0.7978845608028654
GELU_A = 0.044715
MIB = 1 << 20

f32 = jnp.float32
bf16 = jnp.bfloat16


def dot(a, b):
    return jnp.dot(a, b, preferred_element_type=f32)


def dot_t(a, b):
    return lax.dot_general(a, b, (((1,), (1,)), ((), ())), preferred_element_type=f32)


def t_dot(a, b):
    return lax.dot_general(a, b, (((0,), (0,)), ((), ())), preferred_element_type=f32)


def normalize(values):
    mean_v = jnp.mean(values, axis=-1, keepdims=True)
    centered = values - mean_v
    inv_std = lax.rsqrt(jnp.mean(centered * centered, axis=-1, keepdims=True) + EPS)
    return (centered * inv_std, inv_std)


def normalize_back(unit, inv_std, upstream):
    return inv_std * (
        upstream
        - jnp.mean(upstream, axis=-1, keepdims=True)
        - unit * jnp.mean(upstream * unit, axis=-1, keepdims=True)
    )


def halves(rows):
    left = lax.broadcasted_iota(jnp.int32, rows.shape, 1) < HEAD
    zero = jnp.zeros_like(rows)
    return jnp.concatenate([jnp.where(left, rows, zero), jnp.where(left, zero, rows)], 0)


def unhalve(both):
    n = both.shape[1] // 2
    first, second = both[:, :n], both[:, n:]
    upper = lax.broadcasted_iota(jnp.int32, first.shape, 0) < HEAD
    return jnp.where(upper, first, second).T


def sent_slots(groups):
    return [range(1 << bit, groups, 2 << bit) for bit in range(groups.bit_length() - 1)]


def fetch(given, held, sem):
    copies = [pltpu.make_async_copy(src, dst, sem.at[i]) for i, (src, dst) in enumerate(zip(given, held))]
    for copy in copies:
        copy.start()
    return copies


def own_kernel(*refs):
    given, held = refs[:5], refs[5:10]
    q_ref, k_ref, v_ref, unit_ref, inv_ref, sem = refs[10:]
    copies = fetch(given, held, sem)
    x_ref, wk_ref, wv_ref, wq_ref, _ = held
    copies[0].wait()
    unit, inv = normalize(x_ref[...].astype(f32))
    unit_ref[...] = unit
    inv_ref[...] = inv
    normed = unit.astype(bf16)
    copies[1].wait()
    k_ref[...] = dot(normed, wk_ref[...]).astype(bf16)
    copies[2].wait()
    v_ref[...] = dot(normed, wv_ref[...]).astype(bf16)
    copies[3].wait()
    q_ref[...] = (dot(normed, wq_ref[...]) * SCALE).astype(bf16)
    copies[4].wait()


def pair_columns():
    return [(j, slice(j * PAIR, (j + 1) * PAIR)) for j in range(H // 2)]


def early_kernel(
    near_a, q_ref, k_ref, v_ref, wk_ref, wv_ref, cot_ref, wdown_ref, ke_ref, ve_ref, se_ref, gact_ref
):
    rows = q_ref.shape[0]
    unit, _ = normalize(near_a[...].astype(f32))
    normed = unit.astype(bf16)
    ke_ref[:rows, :] = k_ref[...]
    ve_ref[:rows, :] = v_ref[...]
    ke_ref[rows:, :] = dot(normed, wk_ref[...]).astype(bf16)
    ve_ref[rows:, :] = dot(normed, wv_ref[...]).astype(bf16)
    for j, cols in pair_columns():
        se_ref[j] = dot_t(ke_ref[:, cols], halves(q_ref[:, cols]))
    gact_ref[...] = dot_t(cot_ref[...], wdown_ref[...])


def block_back(v, q2, g2, weights, inv, row):
    probs = weights * inv
    ds = (probs * (dot_t(v, g2) - row)).astype(bf16)
    return ds, dot(ds, q2).astype(bf16), dot(probs.astype(bf16), g2).astype(bf16)


def delta_row(delta, j):
    return jnp.concatenate([delta[2 * j : 2 * j + 1, :], delta[2 * j + 1 : 2 * j + 2, :]], 1)


def main_kernel(groups, listed, *refs):
    experts_ref = refs[0]
    slots = refs[1 : 1 + groups]
    (near_b, x_ref, ke_ref, ve_ref, se_ref, q_ref, wk_ref, wv_ref) = refs[1 + groups : 9 + groups]
    (wout_ref, wup_ref, cot_ref, gact_ref) = refs[9 + groups : 13 + groups]
    outs = refs[13 + groups :]
    (send_a, send_b, keep, w_ref, inv_ref, gmixed_ref, delta_ref, kb_ref, vb_ref, ds_ref) = outs[:10]
    (act_ref, resid_ref, gres_ref), outs = outs[10:13], outs[13:]
    bits = groups.bit_length() - 1
    sends = outs[:bits]
    normed_s, mixed_s, gk_s, gv_s = outs[bits:]
    rows, width = x_ref.shape
    early = 2 * rows
    place = lax.axis_index("blk")
    normed_s[:rows, :] = normalize(near_b[...].astype(f32))[0].astype(bf16)
    for e in range(listed):
        slot = experts_ref[:, e : e + 1] ^ place
        block = jnp.zeros((rows, width), f32)
        for i in range(groups):
            block = jnp.where(slot == i, slots[i][...].astype(f32), block)
        normed_s[(1 + e) * rows : (2 + e) * rows, :] = normalize(block)[0].astype(bf16)
    normed = normed_s[...]
    kb_ref[...] = dot(normed, wk_ref[...]).astype(bf16)
    vb_ref[...] = dot(normed, wv_ref[...]).astype(bf16)
    for j, cols in pair_columns():
        last = dot_t(kb_ref[:, cols], halves(q_ref[:, cols]))
        first = se_ref[j]
        top = jnp.maximum(jnp.max(first, axis=0, keepdims=True), jnp.max(last, axis=0, keepdims=True))
        first = jnp.exp(first - top)
        last = jnp.exp(last - top)
        inv = 1.0 / (jnp.sum(first, axis=0, keepdims=True) + jnp.sum(last, axis=0, keepdims=True))
        w_ref[j, :early, :] = first
        w_ref[j, early:, :] = last
        inv_ref[j] = inv
        mixed = t_dot(ve_ref[:, cols], first.astype(bf16)) + t_dot(vb_ref[:, cols], last.astype(bf16))
        mixed_s[:, cols] = unhalve(mixed * inv).astype(bf16)

    mixed = mixed_s[...]
    resid = x_ref[...].astype(f32) + dot(mixed, wout_ref[...])
    resid_ref[...] = resid
    unit2, inv2 = normalize(resid)
    pre = dot(unit2.astype(bf16), wup_ref[...])
    square = pre * pre
    tanh = jnp.tanh(GELU_C * pre * (1.0 + GELU_A * square))
    act_ref[...] = (0.5 * pre * (1.0 + tanh)).astype(bf16)
    slope = 0.5 * (1.0 + tanh) + (0.5 * GELU_C) * pre * (1.0 - tanh * tanh) * (
        1.0 + (3.0 * GELU_A) * square
    )
    gpre = (gact_ref[...] * slope).astype(bf16)
    gres = cot_ref[...].astype(f32) + normalize_back(unit2, inv2, dot_t(gpre, wup_ref[...]))
    gres_ref[...] = gres
    gmixed = dot_t(gres.astype(bf16), wout_ref[...]).astype(bf16)
    gmixed_ref[...] = gmixed
    prod = gmixed.astype(f32) * mixed.astype(f32)
    high = prod.astype(bf16)
    low = (prod - high.astype(f32)).astype(bf16)
    head_of = lax.broadcasted_iota(jnp.int32, (H, width), 1) // HEAD
    ones = (head_of == lax.broadcasted_iota(jnp.int32, (H, width), 0)).astype(bf16)
    delta = dot_t(ones, high) + dot_t(ones, low)
    delta_ref[...] = delta

    for j, cols in pair_columns():
        ds_ref[j], gk_s[:, cols], gv_s[:, cols] = block_back(
            jnp.concatenate([ve_ref[rows:, cols], vb_ref[:, cols]], 0),
            halves(q_ref[:, cols]),
            halves(gmixed[:, cols]),
            w_ref[j, rows:, :],
            inv_ref[j],
            delta_row(delta, j),
        )
    parts = dot_t(gk_s[...], wk_ref[...]) + dot_t(gv_s[...], wv_ref[...])
    send_a[...] = parts[:rows].astype(bf16)
    send_b[...] = parts[rows : 2 * rows].astype(bf16)
    picked = [experts_ref[:, e : e + 1] ^ place for e in range(listed)]

    def far(slot):
        total = jnp.zeros((rows, width), f32)
        for e in range(listed):
            total = total + jnp.where(picked[e] == slot, parts[(2 + e) * rows : (3 + e) * rows], 0.0)
        return total

    keep[...] = far(0)
    for bit, slots_sent in enumerate(sent_slots(groups)):
        for i, slot in enumerate(slots_sent):
            sends[bit][i * rows : (i + 1) * rows, :] = far(slot).astype(bf16)


def rest_kernel(*refs):
    (w_ref, inv_ref, delta_ref, gmixed_ref, q_ref, ke_ref, ve_ref, kb_ref, ds_ref) = refs[:9]
    (keep_ref, act_ref, resid_ref, wq_ref, wk_ref, wv_ref, wdown_ref, out_ref, acc_ref) = refs[9:18]
    gq_s, gk_s, gv_s = refs[18:]
    rows = q_ref.shape[0]
    delta = delta_ref[...]
    for j, cols in pair_columns():
        ds, gk_s[:, cols], gv_s[:, cols] = block_back(
            ve_ref[:rows, cols],
            halves(q_ref[:, cols]),
            halves(gmixed_ref[:, cols]),
            w_ref[j, :rows, :],
            inv_ref[j],
            delta_row(delta, j),
        )
        total = t_dot(ke_ref[:rows, cols], ds) + t_dot(ke_ref[rows:, cols], ds_ref[j, :rows, :])
        total = total + t_dot(kb_ref[:, cols], ds_ref[j, rows:, :])
        gq_s[:, cols] = (unhalve(total) * SCALE).astype(bf16)
    acc_ref[...] = (
        keep_ref[...] + dot_t(gq_s[...], wq_ref[...]) + dot_t(gk_s[...], wk_ref[...]) + dot_t(gv_s[...], wv_ref[...])
    )
    out_ref[...] = (resid_ref[...] + dot(act_ref[...], wdown_ref[...])).astype(bf16)


def last_kernel(unit_ref, inv_ref, gres_ref, acc_ref, *refs):
    out_ref = refs[-1]
    rows = unit_ref.shape[0]
    total = acc_ref[...]
    for part in refs[:-1]:
        total = total + part[:rows, :].astype(f32)
    out_ref[...] = (gres_ref[...] + normalize_back(unit_ref[...], inv_ref[...], total)).astype(bf16)


def call(kernel, outs, args, scratch=(), flops=0, hbm=0):
    spaces = [pltpu.VMEM] * (len(args) - hbm) + [pltpu.HBM] * hbm
    return pl.pallas_call(
        kernel,
        out_shape=[jax.ShapeDtypeStruct(shape, dtype) for shape, dtype in outs],
        in_specs=[pl.BlockSpec(memory_space=space) for space in spaces],
        out_specs=[pl.BlockSpec(memory_space=pltpu.VMEM)] * len(outs),
        scratch_shapes=list(scratch),
        compiler_params=pltpu.CompilerParams(vmem_limit_bytes=40 * MIB),
        cost_estimate=pl.CostEstimate(flops=flops, bytes_accessed=4 * MIB, transcendentals=0),
    )(*args)


def on_device(nodes, experts_list, w_query, w_key, w_value, w_out, w_up, w_down, cotangent):
    rows, width = nodes.shape
    hidden = w_up.shape[1]
    groups = lax.axis_size("blk")
    domains = lax.axis_size("dom")
    listed = experts_list.shape[1]
    bits = groups.bit_length() - 1

    def across(array, bit):
        return lax.ppermute(array, "blk", [(i, i ^ (1 << bit)) for i in range(groups)])

    pairs_a = [(i, i ^ 1) for i in range(domains)]
    pairs_b = []
    for i in range(1, domains, 2):
        pairs_b += [(i, (i + 1) % domains), ((i + 1) % domains, i)]

    held = {0: nodes}
    top = bits - 1
    held[1 << top] = across(nodes, top)
    near_a = lax.ppermute(nodes, "dom", pairs_a)
    near_b = lax.ppermute(nodes, "dom", pairs_b)
    for bit in range(top - 1, -1, -1):
        held = dict(zip(held, lax.optimization_barrier(tuple(held.values()))))
        for slot in list(held):
            held[slot | (1 << bit)] = across(held[slot], bit)

    def in_hbm(*arrays):
        return [pltpu.with_memory_space_constraint(array, pltpu.HBM) for array in arrays]

    given = [nodes, w_key, w_value, w_query, cotangent]
    x, w_key, w_value, w_query, cotangent, q, k, v, unit, inv_std = call(
        own_kernel,
        [(array.shape, array.dtype) for array in given]
        + [((rows, width), bf16)] * 3
        + [((rows, width), f32), ((rows, 1), f32)],
        in_hbm(*given),
        [pltpu.SemaphoreType.DMA((len(given),))],
        flops=6 * rows * width * width,
        hbm=len(given),
    )
    held[0] = x
    early = 2 * rows
    late = (1 + listed) * rows
    keys = early + late
    ke, ve, se, gact = call(
        early_kernel,
        [((early, width), bf16)] * 2 + [((H // 2, early, 2 * rows), f32), ((rows, hidden), f32)],
        [near_a, q, k, v, w_key, w_value, cotangent, w_down],
        flops=2 * early * width * (2 * width + 2 * rows),
    )
    sent = sent_slots(groups)
    send_a, send_b, keep, w, inv, gmixed, delta, kb, vb, ds, act, resid, gres, *sends = call(
        functools.partial(main_kernel, groups, listed),
        [((rows, width), bf16), ((rows, width), bf16), ((rows, width), f32)]
        + [((H // 2, keys, 2 * rows), f32), ((H // 2, 1, 2 * rows), f32)]
        + [((rows, width), bf16), ((H, rows), f32), ((late, width), bf16), ((late, width), bf16)]
        + [((H // 2, keys - rows, 2 * rows), bf16), ((rows, hidden), bf16)]
        + [((rows, width), f32)] * 2
        + [((len(slots) * rows, width), bf16) for slots in sent],
        [experts_list]
        + [held[slot] for slot in range(groups)]
        + [near_b, x, ke, ve, se, q, w_key, w_value]
        + [w_out, w_up, cotangent, gact],
        [pltpu.VMEM((late, width), bf16), pltpu.VMEM((rows, width), bf16)]
        + [pltpu.VMEM((keys - rows, width), bf16)] * 2,
        flops=2 * rows * width * (8 * keys + 4 * hidden),
    )
    from_a = lax.ppermute(send_a, "dom", pairs_a)
    received = [across(sends[0], 0)]
    from_b = lax.ppermute(send_b, "dom", pairs_b)
    for bit in range(1, bits):
        total = sends[bit].astype(f32)
        for lower, array in enumerate(received):
            blocks = array.reshape(-1, rows, width)[(1 << bit) >> (lower + 1) :: (2 << bit) >> (lower + 1)]
            total = total + blocks.reshape(-1, width).astype(f32)
        received.append(across(total.astype(bf16), bit))

    layer_out, acc = call(
        rest_kernel,
        [((rows, width), bf16), ((rows, width), f32)],
        [w, inv, delta, gmixed, q, ke, ve, kb, ds, keep, act, resid, w_query, w_key, w_value, w_down],
        [pltpu.VMEM((rows, width), bf16)] * 3,
        flops=2 * rows * width * (3 * width + hidden + 8 * rows),
    )
    (grad_nodes,) = call(
        last_kernel,
        [((rows, width), bf16)],
        [unit, inv_std, gres, acc, from_a, from_b] + received,
    )
    return (layer_out, grad_nodes)


def solution(mesh):
    split = P(("blk", "dom"), None)
    return jax.shard_map(
        on_device,
        mesh=mesh,
        in_specs=(split, split, P(), P(), P(), P(), P(), P(), split),
        out_specs=(split, split),
        check_vma=False,
    )
```

```python
import functools

import jax
import jax.numpy as jnp
from jax import lax
from jax.experimental import pallas as pl
from jax.experimental.pallas import tpu as pltpu
from jax.sharding import PartitionSpec as P

H = 8
HEAD = 64
EPS = 1e-05
SCALE = HEAD ** (-0.5)
PAIR = 2 * HEAD
GELU_C = 0.7978845608028654
GELU_A = 0.044715
MIB = 1 << 20

f32 = jnp.float32
bf16 = jnp.bfloat16


def dot(a, b):
    return jnp.dot(a, b, preferred_element_type=f32)


def dot_t(a, b):
    return lax.dot_general(a, b, (((1,), (1,)), ((), ())), preferred_element_type=f32)


def t_dot(a, b):
    return lax.dot_general(a, b, (((0,), (0,)), ((), ())), preferred_element_type=f32)


def normalize(values):
    mean_v = jnp.mean(values, axis=-1, keepdims=True)
    centered = values - mean_v
    inv_std = lax.rsqrt(jnp.mean(centered * centered, axis=-1, keepdims=True) + EPS)
    return (centered * inv_std, inv_std)


def normalize_back(unit, inv_std, upstream):
    return inv_std * (
        upstream
        - jnp.mean(upstream, axis=-1, keepdims=True)
        - unit * jnp.mean(upstream * unit, axis=-1, keepdims=True)
    )


def halves(rows):
    left = lax.broadcasted_iota(jnp.int32, rows.shape, 1) < HEAD
    zero = jnp.zeros_like(rows)
    return jnp.concatenate([jnp.where(left, rows, zero), jnp.where(left, zero, rows)], 0)


def unhalve(both):
    n = both.shape[1] // 2
    first, second = both[:, :n], both[:, n:]
    upper = lax.broadcasted_iota(jnp.int32, first.shape, 0) < HEAD
    return jnp.where(upper, first, second).T


def sent_slots(groups):
    return [range(1 << bit, groups, 2 << bit) for bit in range(groups.bit_length() - 1)]


def fetch(given, held, sem):
    copies = [pltpu.make_async_copy(src, dst, sem.at[i]) for i, (src, dst) in enumerate(zip(given, held))]
    for copy in copies:
        copy.start()
    return copies


def own_kernel(*refs):
    given, held = refs[:5], refs[5:10]
    q_ref, k_ref, v_ref, unit_ref, inv_ref, sem = refs[10:]
    copies = fetch(given, held, sem)
    x_ref, wk_ref, wv_ref, wq_ref, _ = held
    copies[0].wait()
    unit, inv = normalize(x_ref[...].astype(f32))
    unit_ref[...] = unit
    inv_ref[...] = inv
    normed = unit.astype(bf16)
    copies[1].wait()
    k_ref[...] = dot(normed, wk_ref[...]).astype(bf16)
    copies[2].wait()
    v_ref[...] = dot(normed, wv_ref[...]).astype(bf16)
    copies[3].wait()
    q_ref[...] = (dot(normed, wq_ref[...]) * SCALE).astype(bf16)
    copies[4].wait()


def pair_columns():
    return [(j, slice(j * PAIR, (j + 1) * PAIR)) for j in range(H // 2)]


def early_kernel(
    near_a, q_ref, k_ref, v_ref, wk_ref, wv_ref, cot_ref, wdown_ref, ke_ref, ve_ref, se_ref, gact_ref
):
    rows = q_ref.shape[0]
    unit, _ = normalize(near_a[...].astype(f32))
    normed = unit.astype(bf16)
    ke_ref[:rows, :] = k_ref[...]
    ve_ref[:rows, :] = v_ref[...]
    ke_ref[rows:, :] = dot(normed, wk_ref[...]).astype(bf16)
    ve_ref[rows:, :] = dot(normed, wv_ref[...]).astype(bf16)
    for j, cols in pair_columns():
        se_ref[j] = dot_t(ke_ref[:, cols], halves(q_ref[:, cols]))
    gact_ref[...] = dot_t(cot_ref[...], wdown_ref[...])


def block_back(v, q2, g2, weights, inv, row):
    probs = weights * inv
    ds = (probs * (dot_t(v, g2) - row)).astype(bf16)
    return ds, dot(ds, q2).astype(bf16), dot(probs.astype(bf16), g2).astype(bf16)


def delta_row(delta, j):
    return jnp.concatenate([delta[2 * j : 2 * j + 1, :], delta[2 * j + 1 : 2 * j + 2, :]], 1)


def main_kernel(groups, listed, *refs):
    experts_ref = refs[0]
    near_b = refs[3]
    slots = refs[1:2] + refs[1 + groups : 3 : -1] + refs[2:3]
    (x_ref, ke_ref, ve_ref, se_ref, q_ref, wk_ref, wv_ref) = refs[2 + groups : 9 + groups]
    (wout_ref, wup_ref, cot_ref, gact_ref) = refs[9 + groups : 13 + groups]
    outs = refs[13 + groups :]
    (send_a, send_b, keep, w_ref, inv_ref, gmixed_ref, delta_ref, kb_ref, vb_ref, ds_ref) = outs[:10]
    (act_ref, resid_ref, gres_ref), outs = outs[10:13], outs[13:]
    bits = groups.bit_length() - 1
    sends = outs[:bits]
    normed_s, mixed_s, gk_s, gv_s = outs[bits:]
    rows, width = x_ref.shape
    early = 2 * rows
    place = lax.axis_index("blk")
    normed_s[:rows, :] = normalize(near_b[...].astype(f32))[0].astype(bf16)
    for e in range(listed):
        slot = experts_ref[:, e : e + 1] ^ place
        block = jnp.zeros((rows, width), f32)
        for i in range(groups):
            block = jnp.where(slot == i, slots[i][...].astype(f32), block)
        normed_s[(1 + e) * rows : (2 + e) * rows, :] = normalize(block)[0].astype(bf16)
    normed = normed_s[...]
    kb_ref[...] = dot(normed, wk_ref[...]).astype(bf16)
    vb_ref[...] = dot(normed, wv_ref[...]).astype(bf16)
    for j, cols in pair_columns():
        last = dot_t(kb_ref[:, cols], halves(q_ref[:, cols]))
        first = se_ref[j]
        top = jnp.maximum(jnp.max(first, axis=0, keepdims=True), jnp.max(last, axis=0, keepdims=True))
        first = jnp.exp(first - top)
        last = jnp.exp(last - top)
        inv = 1.0 / (jnp.sum(first, axis=0, keepdims=True) + jnp.sum(last, axis=0, keepdims=True))
        w_ref[j, :early, :] = first
        w_ref[j, early:, :] = last
        inv_ref[j] = inv
        mixed = t_dot(ve_ref[:, cols], first.astype(bf16)) + t_dot(vb_ref[:, cols], last.astype(bf16))
        mixed_s[:, cols] = unhalve(mixed * inv).astype(bf16)

    mixed = mixed_s[...]
    resid = x_ref[...].astype(f32) + dot(mixed, wout_ref[...])
    resid_ref[...] = resid
    unit2, inv2 = normalize(resid)
    pre = dot(unit2.astype(bf16), wup_ref[...])
    square = pre * pre
    tanh = jnp.tanh(GELU_C * pre * (1.0 + GELU_A * square))
    act_ref[...] = (0.5 * pre * (1.0 + tanh)).astype(bf16)
    slope = 0.5 * (1.0 + tanh) + (0.5 * GELU_C) * pre * (1.0 - tanh * tanh) * (
        1.0 + (3.0 * GELU_A) * square
    )
    gpre = (gact_ref[...] * slope).astype(bf16)
    gres = cot_ref[...].astype(f32) + normalize_back(unit2, inv2, dot_t(gpre, wup_ref[...]))
    gres_ref[...] = gres
    gmixed = dot_t(gres.astype(bf16), wout_ref[...]).astype(bf16)
    gmixed_ref[...] = gmixed
    prod = gmixed.astype(f32) * mixed.astype(f32)
    high = prod.astype(bf16)
    low = (prod - high.astype(f32)).astype(bf16)
    head_of = lax.broadcasted_iota(jnp.int32, (H, width), 1) // HEAD
    ones = (head_of == lax.broadcasted_iota(jnp.int32, (H, width), 0)).astype(bf16)
    delta = dot_t(ones, high) + dot_t(ones, low)
    delta_ref[...] = delta

    for j, cols in pair_columns():
        ds_ref[j], gk_s[:, cols], gv_s[:, cols] = block_back(
            jnp.concatenate([ve_ref[rows:, cols], vb_ref[:, cols]], 0),
            halves(q_ref[:, cols]),
            halves(gmixed[:, cols]),
            w_ref[j, rows:, :],
            inv_ref[j],
            delta_row(delta, j),
        )
    parts = dot_t(gk_s[...], wk_ref[...]) + dot_t(gv_s[...], wv_ref[...])
    send_a[...] = parts[:rows].astype(bf16)
    send_b[...] = parts[rows : 2 * rows].astype(bf16)
    picked = [experts_ref[:, e : e + 1] ^ place for e in range(listed)]

    def far(slot):
        total = jnp.zeros((rows, width), f32)
        for e in range(listed):
            total = total + jnp.where(picked[e] == slot, parts[(2 + e) * rows : (3 + e) * rows], 0.0)
        return total

    keep[...] = far(0)
    for bit, slots_sent in enumerate(sent_slots(groups)):
        for i, slot in enumerate(slots_sent):
            sends[bit][i * rows : (i + 1) * rows, :] = far(slot).astype(bf16)


def rest_kernel(*refs):
    (w_ref, inv_ref, delta_ref, gmixed_ref, q_ref, ke_ref, ve_ref, kb_ref, ds_ref) = refs[:9]
    (keep_ref, act_ref, resid_ref, wq_ref, wk_ref, wv_ref, wdown_ref, out_ref, acc_ref) = refs[9:18]
    gq_s, gk_s, gv_s = refs[18:]
    rows = q_ref.shape[0]
    delta = delta_ref[...]
    for j, cols in pair_columns():
        ds, gk_s[:, cols], gv_s[:, cols] = block_back(
            ve_ref[:rows, cols],
            halves(q_ref[:, cols]),
            halves(gmixed_ref[:, cols]),
            w_ref[j, :rows, :],
            inv_ref[j],
            delta_row(delta, j),
        )
        total = t_dot(ke_ref[:rows, cols], ds) + t_dot(ke_ref[rows:, cols], ds_ref[j, :rows, :])
        total = total + t_dot(kb_ref[:, cols], ds_ref[j, rows:, :])
        gq_s[:, cols] = (unhalve(total) * SCALE).astype(bf16)
    acc_ref[...] = (
        keep_ref[...] + dot_t(gq_s[...], wq_ref[...]) + dot_t(gk_s[...], wk_ref[...]) + dot_t(gv_s[...], wv_ref[...])
    )
    out_ref[...] = (resid_ref[...] + dot(act_ref[...], wdown_ref[...])).astype(bf16)


def last_kernel(unit_ref, inv_ref, gres_ref, acc_ref, *refs):
    out_ref = refs[-1]
    rows = unit_ref.shape[0]
    total = acc_ref[...]
    for part in refs[:-1]:
        total = total + part[:rows, :].astype(f32)
    out_ref[...] = (gres_ref[...] + normalize_back(unit_ref[...], inv_ref[...], total)).astype(bf16)


def call(kernel, outs, args, scratch=(), flops=0, hbm=0):
    spaces = [pltpu.VMEM] * (len(args) - hbm) + [pltpu.HBM] * hbm
    return pl.pallas_call(
        kernel,
        out_shape=[jax.ShapeDtypeStruct(shape, dtype) for shape, dtype in outs],
        in_specs=[pl.BlockSpec(memory_space=space) for space in spaces],
        out_specs=[pl.BlockSpec(memory_space=pltpu.VMEM)] * len(outs),
        scratch_shapes=list(scratch),
        compiler_params=pltpu.CompilerParams(vmem_limit_bytes=40 * MIB),
        cost_estimate=pl.CostEstimate(flops=flops, bytes_accessed=4 * MIB, transcendentals=0),
    )(*args)


def on_device(nodes, experts_list, w_query, w_key, w_value, w_out, w_up, w_down, cotangent):
    rows, width = nodes.shape
    hidden = w_up.shape[1]
    groups = lax.axis_size("blk")
    domains = lax.axis_size("dom")
    listed = experts_list.shape[1]
    bits = groups.bit_length() - 1

    def exchanged(array, slot):
        return lax.ppermute(array, "blk", [(i, i ^ slot) for i in range(groups)])

    def across(array, bit):
        return exchanged(array, 1 << bit)

    pairs_a = [(i, i ^ 1) for i in range(domains)]
    pairs_b = []
    for i in range(1, domains, 2):
        pairs_b += [(i, (i + 1) % domains), ((i + 1) % domains, i)]

    near_a = lax.ppermute(nodes, "dom", pairs_a)
    near_b = lax.ppermute(nodes, "dom", pairs_b)
    held = {slot: exchanged(nodes, slot) for slot in range(1, groups)}

    def in_hbm(*arrays):
        return [pltpu.with_memory_space_constraint(array, pltpu.HBM) for array in arrays]

    given = [nodes, w_key, w_value, w_query, cotangent]
    x, w_key, w_value, w_query, cotangent, q, k, v, unit, inv_std = call(
        own_kernel,
        [(array.shape, array.dtype) for array in given]
        + [((rows, width), bf16)] * 3
        + [((rows, width), f32), ((rows, 1), f32)],
        in_hbm(*given),
        [pltpu.SemaphoreType.DMA((len(given),))],
        flops=6 * rows * width * width,
        hbm=len(given),
    )
    held[0] = x
    early = 2 * rows
    late = (1 + listed) * rows
    keys = early + late
    ke, ve, se, gact = call(
        early_kernel,
        [((early, width), bf16)] * 2 + [((H // 2, early, 2 * rows), f32), ((rows, hidden), f32)],
        [near_a, q, k, v, w_key, w_value, cotangent, w_down],
        flops=2 * early * width * (2 * width + 2 * rows),
    )
    sent = sent_slots(groups)
    send_a, send_b, keep, w, inv, gmixed, delta, kb, vb, ds, act, resid, gres, *sends = call(
        functools.partial(main_kernel, groups, listed),
        [((rows, width), bf16), ((rows, width), bf16), ((rows, width), f32)]
        + [((H // 2, keys, 2 * rows), f32), ((H // 2, 1, 2 * rows), f32)]
        + [((rows, width), bf16), ((H, rows), f32), ((late, width), bf16), ((late, width), bf16)]
        + [((H // 2, keys - rows, 2 * rows), bf16), ((rows, hidden), bf16)]
        + [((rows, width), f32)] * 2
        + [((len(slots) * rows, width), bf16) for slots in sent],
        [experts_list]
        + [x, held[groups - 1], near_b]
        + [held[slot] for slot in range(groups - 2, 0, -1)]
        + [x, ke, ve, se, q, w_key, w_value]
        + [w_out, w_up, cotangent, gact],
        [pltpu.VMEM((late, width), bf16), pltpu.VMEM((rows, width), bf16)]
        + [pltpu.VMEM((keys - rows, width), bf16)] * 2,
        flops=2 * rows * width * (8 * keys + 4 * hidden),
    )
    from_a = lax.ppermute(send_a, "dom", pairs_a)
    received = [across(sends[0], 0)]
    from_b = lax.ppermute(send_b, "dom", pairs_b)
    for bit in range(1, bits):
        total = sends[bit].astype(f32)
        for lower, array in enumerate(received):
            blocks = array.reshape(-1, rows, width)[(1 << bit) >> (lower + 1) :: (2 << bit) >> (lower + 1)]
            total = total + blocks.reshape(-1, width).astype(f32)
        received.append(across(total.astype(bf16), bit))

    layer_out, acc = call(
        rest_kernel,
        [((rows, width), bf16), ((rows, width), f32)],
        [w, inv, delta, gmixed, q, ke, ve, kb, ds, keep, act, resid, w_query, w_key, w_value, w_down],
        [pltpu.VMEM((rows, width), bf16)] * 3,
        flops=2 * rows * width * (3 * width + hidden + 8 * rows),
    )
    (grad_nodes,) = call(
        last_kernel,
        [((rows, width), bf16)],
        [unit, inv_std, gres, acc, from_a, from_b] + received,
    )
    return (layer_out, grad_nodes)


def solution(mesh):
    split = P(("blk", "dom"), None)
    return jax.shard_map(
        on_device,
        mesh=mesh,
        in_specs=(split, split, P(), P(), P(), P(), P(), P(), split),
        out_specs=(split, split),
        check_vma=False,
    )
```

```python
import functools

import jax
import jax.numpy as jnp
from jax import lax
from jax.experimental import pallas as pl
from jax.experimental.pallas import tpu as pltpu
from jax.sharding import PartitionSpec as P

H = 8
HEAD = 64
EPS = 1e-05
SCALE = HEAD ** (-0.5)
PAIR = 2 * HEAD
GELU_C = 0.7978845608028654
GELU_A = 0.044715
MIB = 1 << 20

f32 = jnp.float32
bf16 = jnp.bfloat16


def dot(a, b):
    return jnp.dot(a, b, preferred_element_type=f32)


def dot_t(a, b):
    return lax.dot_general(a, b, (((1,), (1,)), ((), ())), preferred_element_type=f32)


def t_dot(a, b):
    return lax.dot_general(a, b, (((0,), (0,)), ((), ())), preferred_element_type=f32)


def normalize(values):
    mean_v = jnp.mean(values, axis=-1, keepdims=True)
    centered = values - mean_v
    inv_std = lax.rsqrt(jnp.mean(centered * centered, axis=-1, keepdims=True) + EPS)
    return (centered * inv_std, inv_std)


def normalize_back(unit, inv_std, upstream):
    return inv_std * (
        upstream
        - jnp.mean(upstream, axis=-1, keepdims=True)
        - unit * jnp.mean(upstream * unit, axis=-1, keepdims=True)
    )


def halves(rows):
    left = lax.broadcasted_iota(jnp.int32, rows.shape, 1) < HEAD
    zero = jnp.zeros_like(rows)
    return jnp.concatenate([jnp.where(left, rows, zero), jnp.where(left, zero, rows)], 0)


def halves_t(rows):
    turned = rows.T
    upper = lax.broadcasted_iota(jnp.int32, turned.shape, 0) < HEAD
    zero = jnp.zeros_like(turned)
    return jnp.concatenate([jnp.where(upper, turned, zero), jnp.where(upper, zero, turned)], 1)


def unhalve(both):
    n = both.shape[1] // 2
    first, second = both[:, :n], both[:, n:]
    upper = lax.broadcasted_iota(jnp.int32, first.shape, 0) < HEAD
    return jnp.where(upper, first, second).T


def sent_slots(groups):
    return [range(1 << bit, groups, 2 << bit) for bit in range(groups.bit_length() - 1)]


def fetch(given, held, sem):
    copies = [pltpu.make_async_copy(src, dst, sem.at[i]) for i, (src, dst) in enumerate(zip(given, held))]
    for copy in copies:
        copy.start()
    return copies


def own_kernel(*refs):
    given, held = refs[:5], refs[5:10]
    q_ref, k_ref, v_ref, unit_ref, inv_ref, sem = refs[10:]
    copies = fetch(given, held, sem)
    x_ref, wk_ref, wv_ref, wq_ref, _ = held
    copies[0].wait()
    unit, inv = normalize(x_ref[...].astype(f32))
    unit_ref[...] = unit
    inv_ref[...] = inv
    normed = unit.astype(bf16)
    copies[1].wait()
    k_ref[...] = dot(normed, wk_ref[...]).astype(bf16)
    copies[2].wait()
    v_ref[...] = dot(normed, wv_ref[...]).astype(bf16)
    copies[3].wait()
    q_ref[...] = (dot(normed, wq_ref[...]) * SCALE).astype(bf16)
    copies[4].wait()


def pair_columns():
    return [(j, slice(j * PAIR, (j + 1) * PAIR)) for j in range(H // 2)]


def early_kernel(*refs):
    near_a, q_ref, k_ref, v_ref, wk_ref, wv_ref, cot_ref, wdown_ref, wout_ref, given = refs[:10]
    wup_ref, ke_ref, ve_ref, se_ref, gact_ref, q2t_ref, *turned, sem = refs[10:]
    rows = q_ref.shape[0]
    (copy,) = fetch([given], [wup_ref], sem)
    unit, _ = normalize(near_a[...].astype(f32))
    normed = unit.astype(bf16)
    ke_ref[:rows, :] = k_ref[...]
    ve_ref[:rows, :] = v_ref[...]
    ke_ref[rows:, :] = dot(normed, wk_ref[...]).astype(bf16)
    ve_ref[rows:, :] = dot(normed, wv_ref[...]).astype(bf16)
    for j, cols in pair_columns():
        q2t = halves_t(q_ref[:, cols])
        q2t_ref[j] = q2t
        se_ref[j] = dot(ke_ref[:, cols], q2t)
    gact_ref[...] = dot_t(cot_ref[...], wdown_ref[...])
    for weight, out_ref in zip((wk_ref, wv_ref, wout_ref), turned):
        out_ref[...] = weight[...].T
    copy.wait()
    turned[3][...] = wup_ref[...].T


def block_back(v, q, g, weights, inv, row):
    probs = weights * inv
    ds = (probs * (dot(v, halves_t(g)) - row)).astype(bf16)
    return ds, dot(ds, halves(q)).astype(bf16), dot(probs.astype(bf16), halves(g)).astype(bf16)


def delta_row(delta, j):
    return jnp.concatenate([delta[2 * j : 2 * j + 1, :], delta[2 * j + 1 : 2 * j + 2, :]], 1)


def main_kernel(groups, listed, *refs):
    experts_ref = refs[0]
    near_b = refs[3]
    slots = refs[1:2] + refs[1 + groups : 3 : -1] + refs[2:3]
    (x_ref, ve_ref, se_ref, q_ref, q2t_ref, wk_ref, wv_ref) = refs[2 + groups : 9 + groups]
    (wout_ref, wup_ref, cot_ref, gact_ref) = refs[9 + groups : 13 + groups]
    wk_t, wv_t, wout_t, wup_t = refs[13 + groups : 17 + groups]
    outs = refs[17 + groups :]
    (send_a, send_b, keep, w_ref, inv_ref, gmixed_ref, delta_ref, kb_ref, vb_ref, ds_ref) = outs[:10]
    (act_ref, resid_ref, gres_ref), outs = outs[10:13], outs[13:]
    bits = groups.bit_length() - 1
    sends = outs[:bits]
    normed_s, mixed_s, gk_s, gv_s = outs[bits:]
    rows, width = x_ref.shape
    early = ve_ref.shape[0]
    place = lax.axis_index("blk")
    normed_s[:rows, :] = normalize(near_b[...].astype(f32))[0].astype(bf16)
    for e in range(listed):
        slot = experts_ref[:, e : e + 1] ^ place
        block = jnp.zeros((rows, width), f32)
        for i in range(groups):
            block = jnp.where(slot == i, slots[i][...].astype(f32), block)
        normed_s[(1 + e) * rows : (2 + e) * rows, :] = normalize(block)[0].astype(bf16)
    normed = normed_s[...]
    kb_ref[...] = dot(normed, wk_ref[...]).astype(bf16)
    vb_ref[...] = dot(normed, wv_ref[...]).astype(bf16)
    for j, cols in pair_columns():
        last = dot(kb_ref[:, cols], q2t_ref[j])
        first = se_ref[j]
        top = jnp.maximum(jnp.max(first, axis=0, keepdims=True), jnp.max(last, axis=0, keepdims=True))
        first = jnp.exp(first - top)
        last = jnp.exp(last - top)
        inv = 1.0 / (jnp.sum(first, axis=0, keepdims=True) + jnp.sum(last, axis=0, keepdims=True))
        w_ref[j, :early, :] = first
        w_ref[j, early:, :] = last
        inv_ref[j] = inv
        mixed = t_dot(ve_ref[:, cols], first.astype(bf16)) + t_dot(vb_ref[:, cols], last.astype(bf16))
        mixed_s[:, cols] = unhalve(mixed * inv).astype(bf16)

    mixed = mixed_s[...]
    resid = x_ref[...].astype(f32) + dot(mixed, wout_ref[...])
    resid_ref[...] = resid
    unit2, inv2 = normalize(resid)
    pre = dot(unit2.astype(bf16), wup_ref[...])
    square = pre * pre
    tanh = jnp.tanh(GELU_C * pre * (1.0 + GELU_A * square))
    act_ref[...] = (0.5 * pre * (1.0 + tanh)).astype(bf16)
    slope = 0.5 * (1.0 + tanh) + (0.5 * GELU_C) * pre * (1.0 - tanh * tanh) * (
        1.0 + (3.0 * GELU_A) * square
    )
    gpre = (gact_ref[...] * slope).astype(bf16)
    gres = cot_ref[...].astype(f32) + normalize_back(unit2, inv2, dot(gpre, wup_t[...]))
    gres_ref[...] = gres
    gmixed = dot(gres.astype(bf16), wout_t[...]).astype(bf16)
    gmixed_ref[...] = gmixed
    prod = gmixed.astype(f32) * mixed.astype(f32)
    high = prod.astype(bf16)
    low = (prod - high.astype(f32)).astype(bf16)
    head_of = lax.broadcasted_iota(jnp.int32, (H, width), 1) // HEAD
    ones = (head_of == lax.broadcasted_iota(jnp.int32, (H, width), 0)).astype(bf16)
    delta = dot_t(ones, high) + dot_t(ones, low)
    delta_ref[...] = delta

    for j, cols in pair_columns():
        ds_ref[j], gk_s[:, cols], gv_s[:, cols] = block_back(
            jnp.concatenate([ve_ref[rows:, cols], vb_ref[:, cols]], 0),
            q_ref[:, cols],
            gmixed[:, cols],
            w_ref[j, rows:, :],
            inv_ref[j],
            delta_row(delta, j),
        )
    parts = dot(gk_s[...], wk_t[...]) + dot(gv_s[...], wv_t[...])
    send_a[...] = parts[:rows].astype(bf16)
    send_b[...] = parts[rows : 2 * rows].astype(bf16)
    picked = [experts_ref[:, e : e + 1] ^ place for e in range(listed)]

    def far(slot):
        total = jnp.zeros((rows, width), f32)
        for e in range(listed):
            total = total + jnp.where(picked[e] == slot, parts[(2 + e) * rows : (3 + e) * rows], 0.0)
        return total

    keep[...] = far(0)
    for bit, slots_sent in enumerate(sent_slots(groups)):
        for i, slot in enumerate(slots_sent):
            sends[bit][i * rows : (i + 1) * rows, :] = far(slot).astype(bf16)


def rest_kernel(*refs):
    (w_ref, inv_ref, delta_ref, gmixed_ref, q_ref, ke_ref, ve_ref, kb_ref, ds_ref) = refs[:9]
    (keep_ref, act_ref, resid_ref, wq_ref, wk_ref, wv_ref, wdown_ref, out_ref, acc_ref) = refs[9:18]
    gq_s, gk_s, gv_s = refs[18:]
    rows = q_ref.shape[0]
    delta = delta_ref[...]
    for j, cols in pair_columns():
        ds, gk_s[:, cols], gv_s[:, cols] = block_back(
            ve_ref[:rows, cols],
            q_ref[:, cols],
            gmixed_ref[:, cols],
            w_ref[j, :rows, :],
            inv_ref[j],
            delta_row(delta, j),
        )
        total = t_dot(ke_ref[:rows, cols], ds) + t_dot(ke_ref[rows:, cols], ds_ref[j, :rows, :])
        total = total + t_dot(kb_ref[:, cols], ds_ref[j, rows:, :])
        gq_s[:, cols] = (unhalve(total) * SCALE).astype(bf16)
    acc_ref[...] = (
        keep_ref[...] + dot_t(gq_s[...], wq_ref[...]) + dot(gk_s[...], wk_ref[...]) + dot(gv_s[...], wv_ref[...])
    )
    out_ref[...] = (resid_ref[...] + dot(act_ref[...], wdown_ref[...])).astype(bf16)


def last_kernel(unit_ref, inv_ref, gres_ref, acc_ref, *refs):
    out_ref = refs[-1]
    rows = unit_ref.shape[0]
    total = acc_ref[...]
    for part in refs[:-1]:
        total = total + part[:rows, :].astype(f32)
    out_ref[...] = (gres_ref[...] + normalize_back(unit_ref[...], inv_ref[...], total)).astype(bf16)


def call(kernel, outs, args, scratch=(), flops=0, hbm=0):
    spaces = [pltpu.VMEM] * (len(args) - hbm) + [pltpu.HBM] * hbm
    return pl.pallas_call(
        kernel,
        out_shape=[jax.ShapeDtypeStruct(shape, dtype) for shape, dtype in outs],
        in_specs=[pl.BlockSpec(memory_space=space) for space in spaces],
        out_specs=[pl.BlockSpec(memory_space=pltpu.VMEM)] * len(outs),
        scratch_shapes=list(scratch),
        compiler_params=pltpu.CompilerParams(vmem_limit_bytes=40 * MIB),
        cost_estimate=pl.CostEstimate(flops=flops, bytes_accessed=4 * MIB, transcendentals=0),
    )(*args)


def on_device(nodes, experts_list, w_query, w_key, w_value, w_out, w_up, w_down, cotangent):
    rows, width = nodes.shape
    hidden = w_up.shape[1]
    groups = lax.axis_size("blk")
    domains = lax.axis_size("dom")
    listed = experts_list.shape[1]
    bits = groups.bit_length() - 1

    def exchanged(array, slot):
        return lax.ppermute(array, "blk", [(i, i ^ slot) for i in range(groups)])

    def across(array, bit):
        return exchanged(array, 1 << bit)

    pairs_a = [(i, i ^ 1) for i in range(domains)]
    pairs_b = []
    for i in range(1, domains, 2):
        pairs_b += [(i, (i + 1) % domains), ((i + 1) % domains, i)]

    near_a = lax.ppermute(nodes, "dom", pairs_a)
    near_b = lax.ppermute(nodes, "dom", pairs_b)
    held = {slot: exchanged(nodes, slot) for slot in range(1, groups)}

    def in_hbm(*arrays):
        return [pltpu.with_memory_space_constraint(array, pltpu.HBM) for array in arrays]

    given = [nodes, w_key, w_value, w_query, cotangent]
    x, w_key, w_value, w_query, cotangent, q, k, v, unit, inv_std = call(
        own_kernel,
        [(array.shape, array.dtype) for array in given]
        + [((rows, width), bf16)] * 3
        + [((rows, width), f32), ((rows, 1), f32)],
        in_hbm(*given),
        [pltpu.SemaphoreType.DMA((len(given),))],
        flops=6 * rows * width * width,
        hbm=len(given),
    )
    held[0] = x
    early = 2 * rows
    late = (1 + listed) * rows
    keys = early + late
    w_up, ke, ve, se, gact, q2t, wk_t, wv_t, wout_t, wup_t = call(
        early_kernel,
        [(w_up.shape, bf16)]
        + [((early, width), bf16)] * 2
        + [((H // 2, early, 2 * rows), f32), ((rows, hidden), f32), ((H // 2, PAIR, 2 * rows), bf16)]
        + [((width, width), bf16)] * 3
        + [((hidden, width), bf16)],
        [near_a, q, k, v, w_key, w_value, cotangent, w_down, w_out] + in_hbm(w_up),
        [pltpu.SemaphoreType.DMA((1,))],
        hbm=1,
        flops=2 * early * width * (2 * width + 2 * rows),
    )
    sent = sent_slots(groups)
    send_a, send_b, keep, w, inv, gmixed, delta, kb, vb, ds, act, resid, gres, *sends = call(
        functools.partial(main_kernel, groups, listed),
        [((rows, width), bf16), ((rows, width), bf16), ((rows, width), f32)]
        + [((H // 2, keys, 2 * rows), f32), ((H // 2, 1, 2 * rows), f32)]
        + [((rows, width), bf16), ((H, rows), f32), ((late, width), bf16), ((late, width), bf16)]
        + [((H // 2, keys - rows, 2 * rows), bf16), ((rows, hidden), bf16)]
        + [((rows, width), f32)] * 2
        + [((len(slots) * rows, width), bf16) for slots in sent],
        [experts_list]
        + [x, held[groups - 1], near_b]
        + [held[slot] for slot in range(groups - 2, 0, -1)]
        + [x, ve, se, q, q2t, w_key, w_value]
        + [w_out, w_up, cotangent, gact, wk_t, wv_t, wout_t, wup_t],
        [pltpu.VMEM((late, width), bf16), pltpu.VMEM((rows, width), bf16)]
        + [pltpu.VMEM((keys - rows, width), bf16)] * 2,
        flops=2 * rows * width * (8 * keys + 4 * hidden),
    )
    from_a = lax.ppermute(send_a, "dom", pairs_a)
    received = [across(sends[0], 0)]
    from_b = lax.ppermute(send_b, "dom", pairs_b)
    for bit in range(1, bits):
        total = sends[bit].astype(f32)
        for lower, array in enumerate(received):
            blocks = array.reshape(-1, rows, width)[(1 << bit) >> (lower + 1) :: (2 << bit) >> (lower + 1)]
            total = total + blocks.reshape(-1, width).astype(f32)
        received.append(across(total.astype(bf16), bit))

    layer_out, acc = call(
        rest_kernel,
        [((rows, width), bf16), ((rows, width), f32)],
        [w, inv, delta, gmixed, q, ke, ve, kb, ds, keep, act, resid, w_query, wk_t, wv_t, w_down],
        [pltpu.VMEM((rows, width), bf16)] * 3,
        flops=2 * rows * width * (3 * width + hidden + 8 * rows),
    )
    (grad_nodes,) = call(
        last_kernel,
        [((rows, width), bf16)],
        [unit, inv_std, gres, acc, from_a, from_b] + received,
    )
    return (layer_out, grad_nodes)


def solution(mesh):
    split = P(("blk", "dom"), None)
    return jax.shard_map(
        on_device,
        mesh=mesh,
        in_specs=(split, split, P(), P(), P(), P(), P(), P(), split),
        out_specs=(split, split),
        check_vma=False,
    )
```

```python
import functools

import jax
import jax.numpy as jnp
from jax import lax
from jax.experimental import pallas as pl
from jax.experimental.pallas import tpu as pltpu
from jax.sharding import PartitionSpec as P

H = 8
HEAD = 64
EPS = 1e-05
SCALE = HEAD ** (-0.5)
PAIR = 2 * HEAD
GELU_C = 0.7978845608028654
GELU_A = 0.044715
MIB = 1 << 20

f32 = jnp.float32
bf16 = jnp.bfloat16


def dot(a, b):
    return jnp.dot(a, b, preferred_element_type=f32)


def dot_t(a, b):
    return lax.dot_general(a, b, (((1,), (1,)), ((), ())), preferred_element_type=f32)


def t_dot(a, b):
    return lax.dot_general(a, b, (((0,), (0,)), ((), ())), preferred_element_type=f32)


def normalize(values):
    mean_v = jnp.mean(values, axis=-1, keepdims=True)
    centered = values - mean_v
    inv_std = lax.rsqrt(jnp.mean(centered * centered, axis=-1, keepdims=True) + EPS)
    return (centered * inv_std, inv_std)


def normalize_back(unit, inv_std, upstream):
    return inv_std * (
        upstream
        - jnp.mean(upstream, axis=-1, keepdims=True)
        - unit * jnp.mean(upstream * unit, axis=-1, keepdims=True)
    )


def halves(rows):
    left = lax.broadcasted_iota(jnp.int32, rows.shape, 1) < HEAD
    zero = jnp.zeros_like(rows)
    return jnp.concatenate([jnp.where(left, rows, zero), jnp.where(left, zero, rows)], 0)


def halves_t(rows):
    turned = rows.T
    upper = lax.broadcasted_iota(jnp.int32, turned.shape, 0) < HEAD
    zero = jnp.zeros_like(turned)
    return jnp.concatenate([jnp.where(upper, turned, zero), jnp.where(upper, zero, turned)], 1)


def unhalve(both):
    n = both.shape[1] // 2
    first, second = both[:, :n], both[:, n:]
    upper = lax.broadcasted_iota(jnp.int32, first.shape, 0) < HEAD
    return jnp.where(upper, first, second).T


def sent_slots(groups):
    return [range(1 << bit, groups, 2 << bit) for bit in range(groups.bit_length() - 1)]


def fetch(given, held, sem):
    copies = [pltpu.make_async_copy(src, dst, sem.at[i]) for i, (src, dst) in enumerate(zip(given, held))]
    for copy in copies:
        copy.start()
    return copies


def own_kernel(*refs):
    given, held = refs[:6], refs[6:12]
    q_ref, k_ref, v_ref, unit_ref, inv_ref, sem = refs[12:]
    copies = fetch(given, held, sem)
    x_ref, wk_ref, wv_ref, wq_ref = held[:4]
    copies[0].wait()
    unit, inv = normalize(x_ref[...].astype(f32))
    unit_ref[...] = unit
    inv_ref[...] = inv
    normed = unit.astype(bf16)
    copies[1].wait()
    k_ref[...] = dot(normed, wk_ref[...]).astype(bf16)
    copies[2].wait()
    v_ref[...] = dot(normed, wv_ref[...]).astype(bf16)
    copies[3].wait()
    q_ref[...] = (dot(normed, wq_ref[...]) * SCALE).astype(bf16)
    copies[4].wait()
    copies[5].wait()


def pair_columns():
    return [(j, slice(j * PAIR, (j + 1) * PAIR)) for j in range(H // 2)]


def early_kernel(*refs):
    near_a, q_ref, k_ref, v_ref, wk_ref, wv_ref, cot_ref, wdown_ref, wout_ref, wup_ref = refs[:10]
    ke_ref, ve_ref, se_ref, gact_ref, q2t_ref, *turned = refs[10:]
    rows = q_ref.shape[0]
    unit, _ = normalize(near_a[...].astype(f32))
    normed = unit.astype(bf16)
    ke_ref[:rows, :] = k_ref[...]
    ve_ref[:rows, :] = v_ref[...]
    ke_ref[rows:, :] = dot(normed, wk_ref[...]).astype(bf16)
    ve_ref[rows:, :] = dot(normed, wv_ref[...]).astype(bf16)
    for j, cols in pair_columns():
        q2t = halves_t(q_ref[:, cols])
        q2t_ref[j] = q2t
        se_ref[j] = dot(ke_ref[:, cols], q2t)
    gact_ref[...] = dot_t(cot_ref[...], wdown_ref[...])
    for weight, out_ref in zip((wk_ref, wv_ref, wout_ref, wup_ref), turned):
        out_ref[...] = weight[...].T


def block_back(v, q, g, weights, inv, row):
    probs = weights * inv
    ds = (probs * (dot(v, halves_t(g)) - row)).astype(bf16)
    return ds, dot(ds, halves(q)).astype(bf16), dot(probs.astype(bf16), halves(g)).astype(bf16)


def delta_row(delta, j):
    return jnp.concatenate([delta[2 * j : 2 * j + 1, :], delta[2 * j + 1 : 2 * j + 2, :]], 1)


def main_kernel(groups, listed, *refs):
    experts_ref = refs[0]
    near_b = refs[3]
    slots = refs[1:2] + refs[1 + groups : 3 : -1] + refs[2:3]
    (x_ref, ve_ref, se_ref, q_ref, q2t_ref, wk_ref, wv_ref) = refs[2 + groups : 9 + groups]
    (wout_ref, wup_ref, cot_ref, gact_ref) = refs[9 + groups : 13 + groups]
    wk_t, wv_t, wout_t, wup_t = refs[13 + groups : 17 + groups]
    outs = refs[17 + groups :]
    (send_a, send_b, keep, w_ref, inv_ref, gmixed_ref, delta_ref, kb_ref, vb_ref, ds_ref) = outs[:10]
    (act_ref, resid_ref, gres_ref), outs = outs[10:13], outs[13:]
    bits = groups.bit_length() - 1
    sends = outs[:bits]
    normed_s, mixed_s, gk_s, gv_s = outs[bits:]
    rows, width = x_ref.shape
    early = ve_ref.shape[0]
    place = lax.axis_index("blk")
    normed_s[:rows, :] = normalize(near_b[...].astype(f32))[0].astype(bf16)
    for e in range(listed):
        slot = experts_ref[:, e : e + 1] ^ place
        block = jnp.zeros((rows, width), f32)
        for i in range(groups):
            block = jnp.where(slot == i, slots[i][...].astype(f32), block)
        normed_s[(1 + e) * rows : (2 + e) * rows, :] = normalize(block)[0].astype(bf16)
    normed = normed_s[...]
    kb_ref[...] = dot(normed, wk_ref[...]).astype(bf16)
    vb_ref[...] = dot(normed, wv_ref[...]).astype(bf16)
    for j, cols in pair_columns():
        last = dot(kb_ref[:, cols], q2t_ref[j])
        first = se_ref[j]
        top = jnp.maximum(jnp.max(first, axis=0, keepdims=True), jnp.max(last, axis=0, keepdims=True))
        first = jnp.exp(first - top)
        last = jnp.exp(last - top)
        inv = 1.0 / (jnp.sum(first, axis=0, keepdims=True) + jnp.sum(last, axis=0, keepdims=True))
        w_ref[j, :early, :] = first
        w_ref[j, early:, :] = last
        inv_ref[j] = inv
        mixed = t_dot(ve_ref[:, cols], first.astype(bf16)) + t_dot(vb_ref[:, cols], last.astype(bf16))
        mixed_s[:, cols] = unhalve(mixed * inv).astype(bf16)

    mixed = mixed_s[...]
    resid = x_ref[...].astype(f32) + dot(mixed, wout_ref[...])
    resid_ref[...] = resid
    unit2, inv2 = normalize(resid)
    pre = dot(unit2.astype(bf16), wup_ref[...])
    square = pre * pre
    tanh = jnp.tanh(GELU_C * pre * (1.0 + GELU_A * square))
    act_ref[...] = (0.5 * pre * (1.0 + tanh)).astype(bf16)
    slope = 0.5 * (1.0 + tanh) + (0.5 * GELU_C) * pre * (1.0 - tanh * tanh) * (
        1.0 + (3.0 * GELU_A) * square
    )
    gpre = (gact_ref[...] * slope).astype(bf16)
    gres = cot_ref[...].astype(f32) + normalize_back(unit2, inv2, dot(gpre, wup_t[...]))
    gres_ref[...] = gres
    gmixed = dot(gres.astype(bf16), wout_t[...]).astype(bf16)
    gmixed_ref[...] = gmixed
    prod = gmixed.astype(f32) * mixed.astype(f32)
    high = prod.astype(bf16)
    low = (prod - high.astype(f32)).astype(bf16)
    head_of = lax.broadcasted_iota(jnp.int32, (H, width), 1) // HEAD
    ones = (head_of == lax.broadcasted_iota(jnp.int32, (H, width), 0)).astype(bf16)
    delta = dot_t(ones, high) + dot_t(ones, low)
    delta_ref[...] = delta

    for j, cols in pair_columns():
        ds_ref[j], gk_s[:, cols], gv_s[:, cols] = block_back(
            jnp.concatenate([ve_ref[rows:, cols], vb_ref[:, cols]], 0),
            q_ref[:, cols],
            gmixed[:, cols],
            w_ref[j, rows:, :],
            inv_ref[j],
            delta_row(delta, j),
        )
    parts = dot(gk_s[...], wk_t[...]) + dot(gv_s[...], wv_t[...])
    send_a[...] = parts[:rows].astype(bf16)
    send_b[...] = parts[rows : 2 * rows].astype(bf16)
    picked = [experts_ref[:, e : e + 1] ^ place for e in range(listed)]

    def far(slot):
        total = jnp.zeros((rows, width), f32)
        for e in range(listed):
            total = total + jnp.where(picked[e] == slot, parts[(2 + e) * rows : (3 + e) * rows], 0.0)
        return total

    keep[...] = far(0)
    for bit, slots_sent in enumerate(sent_slots(groups)):
        for i, slot in enumerate(slots_sent):
            sends[bit][i * rows : (i + 1) * rows, :] = far(slot).astype(bf16)


def rest_kernel(*refs):
    (w_ref, inv_ref, delta_ref, gmixed_ref, q_ref, ke_ref, ve_ref, kb_ref, ds_ref) = refs[:9]
    (keep_ref, act_ref, resid_ref, wq_ref, wk_ref, wv_ref, wdown_ref, out_ref, acc_ref) = refs[9:18]
    gq_s, gk_s, gv_s = refs[18:]
    rows = q_ref.shape[0]
    delta = delta_ref[...]
    for j, cols in pair_columns():
        ds, gk_s[:, cols], gv_s[:, cols] = block_back(
            ve_ref[:rows, cols],
            q_ref[:, cols],
            gmixed_ref[:, cols],
            w_ref[j, :rows, :],
            inv_ref[j],
            delta_row(delta, j),
        )
        total = t_dot(ke_ref[:rows, cols], ds) + t_dot(ke_ref[rows:, cols], ds_ref[j, :rows, :])
        total = total + t_dot(kb_ref[:, cols], ds_ref[j, rows:, :])
        gq_s[:, cols] = (unhalve(total) * SCALE).astype(bf16)
    acc_ref[...] = (
        keep_ref[...] + dot_t(gq_s[...], wq_ref[...]) + dot(gk_s[...], wk_ref[...]) + dot(gv_s[...], wv_ref[...])
    )
    out_ref[...] = (resid_ref[...] + dot(act_ref[...], wdown_ref[...])).astype(bf16)


def last_kernel(unit_ref, inv_ref, gres_ref, acc_ref, *refs):
    out_ref = refs[-1]
    rows = unit_ref.shape[0]
    total = acc_ref[...]
    for part in refs[:-1]:
        total = total + part[:rows, :].astype(f32)
    out_ref[...] = (gres_ref[...] + normalize_back(unit_ref[...], inv_ref[...], total)).astype(bf16)


def call(kernel, outs, args, scratch=(), flops=0, hbm=0):
    spaces = [pltpu.VMEM] * (len(args) - hbm) + [pltpu.HBM] * hbm
    return pl.pallas_call(
        kernel,
        out_shape=[jax.ShapeDtypeStruct(shape, dtype) for shape, dtype in outs],
        in_specs=[pl.BlockSpec(memory_space=space) for space in spaces],
        out_specs=[pl.BlockSpec(memory_space=pltpu.VMEM)] * len(outs),
        scratch_shapes=list(scratch),
        compiler_params=pltpu.CompilerParams(vmem_limit_bytes=40 * MIB),
        cost_estimate=pl.CostEstimate(flops=flops, bytes_accessed=4 * MIB, transcendentals=0),
    )(*args)


def on_device(nodes, experts_list, w_query, w_key, w_value, w_out, w_up, w_down, cotangent):
    rows, width = nodes.shape
    hidden = w_up.shape[1]
    groups = lax.axis_size("blk")
    domains = lax.axis_size("dom")
    listed = experts_list.shape[1]
    bits = groups.bit_length() - 1

    def exchanged(array, slot):
        return lax.ppermute(array, "blk", [(i, i ^ slot) for i in range(groups)])

    def across(array, bit):
        return exchanged(array, 1 << bit)

    pairs_a = [(i, i ^ 1) for i in range(domains)]
    pairs_b = []
    for i in range(1, domains, 2):
        pairs_b += [(i, (i + 1) % domains), ((i + 1) % domains, i)]

    near_a = lax.ppermute(nodes, "dom", pairs_a)
    near_b = lax.ppermute(nodes, "dom", pairs_b)
    held = {slot: exchanged(nodes, slot) for slot in range(1, groups)}

    def in_hbm(*arrays):
        return [pltpu.with_memory_space_constraint(array, pltpu.HBM) for array in arrays]

    given = [nodes, w_key, w_value, w_query, cotangent, w_up]
    x, w_key, w_value, w_query, cotangent, w_up, q, k, v, unit, inv_std = call(
        own_kernel,
        [(array.shape, array.dtype) for array in given]
        + [((rows, width), bf16)] * 3
        + [((rows, width), f32), ((rows, 1), f32)],
        in_hbm(*given),
        [pltpu.SemaphoreType.DMA((len(given),))],
        flops=6 * rows * width * width,
        hbm=len(given),
    )
    held[0] = x
    early = 2 * rows
    late = (1 + listed) * rows
    keys = early + late
    ke, ve, se, gact, q2t, wk_t, wv_t, wout_t, wup_t = call(
        early_kernel,
        [((early, width), bf16)] * 2
        + [((H // 2, early, 2 * rows), f32), ((rows, hidden), f32), ((H // 2, PAIR, 2 * rows), bf16)]
        + [((width, width), bf16)] * 3
        + [((hidden, width), bf16)],
        [near_a, q, k, v, w_key, w_value, cotangent, w_down, w_out, w_up],
        flops=2 * early * width * (2 * width + 2 * rows),
    )
    sent = sent_slots(groups)
    send_a, send_b, keep, w, inv, gmixed, delta, kb, vb, ds, act, resid, gres, *sends = call(
        functools.partial(main_kernel, groups, listed),
        [((rows, width), bf16), ((rows, width), bf16), ((rows, width), f32)]
        + [((H // 2, keys, 2 * rows), f32), ((H // 2, 1, 2 * rows), f32)]
        + [((rows, width), bf16), ((H, rows), f32), ((late, width), bf16), ((late, width), bf16)]
        + [((H // 2, keys - rows, 2 * rows), bf16), ((rows, hidden), bf16)]
        + [((rows, width), f32)] * 2
        + [((len(slots) * rows, width), bf16) for slots in sent],
        [experts_list]
        + [x, held[groups - 1], near_b]
        + [held[slot] for slot in range(groups - 2, 0, -1)]
        + [x, ve, se, q, q2t, w_key, w_value]
        + [w_out, w_up, cotangent, gact, wk_t, wv_t, wout_t, wup_t],
        [pltpu.VMEM((late, width), bf16), pltpu.VMEM((rows, width), bf16)]
        + [pltpu.VMEM((keys - rows, width), bf16)] * 2,
        flops=2 * rows * width * (8 * keys + 4 * hidden),
    )
    from_a = lax.ppermute(send_a, "dom", pairs_a)
    received = [across(sends[0], 0)]
    from_b = lax.ppermute(send_b, "dom", pairs_b)
    for bit in range(1, bits):
        total = sends[bit].astype(f32)
        for lower, array in enumerate(received):
            blocks = array.reshape(-1, rows, width)[(1 << bit) >> (lower + 1) :: (2 << bit) >> (lower + 1)]
            total = total + blocks.reshape(-1, width).astype(f32)
        received.append(across(total.astype(bf16), bit))

    layer_out, acc = call(
        rest_kernel,
        [((rows, width), bf16), ((rows, width), f32)],
        [w, inv, delta, gmixed, q, ke, ve, kb, ds, keep, act, resid, w_query, wk_t, wv_t, w_down],
        [pltpu.VMEM((rows, width), bf16)] * 3,
        flops=2 * rows * width * (3 * width + hidden + 8 * rows),
    )
    (grad_nodes,) = call(
        last_kernel,
        [((rows, width), bf16)],
        [unit, inv_std, gres, acc, from_a, from_b] + received,
    )
    return (layer_out, grad_nodes)


def solution(mesh):
    split = P(("blk", "dom"), None)
    return jax.shard_map(
        on_device,
        mesh=mesh,
        in_specs=(split, split, P(), P(), P(), P(), P(), P(), split),
        out_specs=(split, split),
        check_vma=False,
    )
```

```python
import functools

import jax
import jax.numpy as jnp
from jax import lax
from jax.experimental import pallas as pl
from jax.experimental.pallas import tpu as pltpu
from jax.sharding import PartitionSpec as P

H = 8
HEAD = 64
EPS = 1e-05
SCALE = HEAD ** (-0.5)
PAIR = 2 * HEAD
GELU_C = 0.7978845608028654
GELU_A = 0.044715
MIB = 1 << 20

f32 = jnp.float32
bf16 = jnp.bfloat16


def dot(a, b):
    return jnp.dot(a, b, preferred_element_type=f32)


def dot_t(a, b):
    return lax.dot_general(a, b, (((1,), (1,)), ((), ())), preferred_element_type=f32)


def t_dot(a, b):
    return lax.dot_general(a, b, (((0,), (0,)), ((), ())), preferred_element_type=f32)


def normalize(values):
    mean_v = jnp.mean(values, axis=-1, keepdims=True)
    centered = values - mean_v
    inv_std = lax.rsqrt(jnp.mean(centered * centered, axis=-1, keepdims=True) + EPS)
    return (centered * inv_std, inv_std)


def normalize_back(unit, inv_std, upstream):
    return inv_std * (
        upstream
        - jnp.mean(upstream, axis=-1, keepdims=True)
        - unit * jnp.mean(upstream * unit, axis=-1, keepdims=True)
    )


def halves(rows):
    left = lax.broadcasted_iota(jnp.int32, rows.shape, 1) < HEAD
    zero = jnp.zeros_like(rows)
    return jnp.concatenate([jnp.where(left, rows, zero), jnp.where(left, zero, rows)], 0)


def halves_t(rows):
    turned = rows.T
    upper = lax.broadcasted_iota(jnp.int32, turned.shape, 0) < HEAD
    zero = jnp.zeros_like(turned)
    return jnp.concatenate([jnp.where(upper, turned, zero), jnp.where(upper, zero, turned)], 1)


def unhalve(both):
    n = both.shape[1] // 2
    first, second = both[:, :n], both[:, n:]
    upper = lax.broadcasted_iota(jnp.int32, first.shape, 0) < HEAD
    return jnp.where(upper, first, second).T


def sent_slots(groups):
    return [range(1 << bit, groups, 2 << bit) for bit in range(groups.bit_length() - 1)]


def fetch(given, held, sem):
    copies = [pltpu.make_async_copy(src, dst, sem.at[i]) for i, (src, dst) in enumerate(zip(given, held))]
    for copy in copies:
        copy.start()
    return copies


def own_kernel(*refs):
    given, held = refs[:6], refs[6:12]
    q_ref, k_ref, v_ref, unit_ref, inv_ref, sem = refs[12:]
    copies = fetch(given, held, sem)
    x_ref, wk_ref, wv_ref, wq_ref = held[:4]
    copies[0].wait()
    unit, inv = normalize(x_ref[...].astype(f32))
    unit_ref[...] = unit
    inv_ref[...] = inv
    normed = unit.astype(bf16)
    copies[1].wait()
    k_ref[...] = dot(normed, wk_ref[...]).astype(bf16)
    copies[2].wait()
    v_ref[...] = dot(normed, wv_ref[...]).astype(bf16)
    copies[3].wait()
    q_ref[...] = (dot(normed, wq_ref[...]) * SCALE).astype(bf16)
    copies[4].wait()
    copies[5].wait()


def pair_columns():
    return [(j, slice(j * PAIR, (j + 1) * PAIR)) for j in range(H // 2)]


def early_kernel(*refs):
    near_a, q_ref, k_ref, v_ref, wk_ref, wv_ref, cot_ref, wdown_ref, wout_ref, wup_ref = refs[:10]
    ke_ref, ve_ref, se_ref, gact_ref, q2t_ref, *turned = refs[10:]
    rows = q_ref.shape[0]
    unit, _ = normalize(near_a[...].astype(f32))
    normed = unit.astype(bf16)
    ke_ref[:rows, :] = k_ref[...]
    ve_ref[:rows, :] = v_ref[...]
    ke_ref[rows:, :] = dot(normed, wk_ref[...]).astype(bf16)
    ve_ref[rows:, :] = dot(normed, wv_ref[...]).astype(bf16)
    for j, cols in pair_columns():
        q2t = halves_t(q_ref[:, cols])
        q2t_ref[j] = q2t
        se_ref[j] = dot(ke_ref[:, cols], q2t)
    gact_ref[...] = dot_t(cot_ref[...], wdown_ref[...])
    for weight, out_ref in zip((wk_ref, wv_ref, wout_ref, wup_ref), turned):
        out_ref[...] = weight[...].T


def block_back(v, q, g, weights, inv, row):
    probs = weights * inv
    ds = (probs * (dot(v, halves_t(g)) - row)).astype(bf16)
    return ds, dot(ds, halves(q)).astype(bf16), dot(probs.astype(bf16), halves(g)).astype(bf16)


def delta_row(delta, j):
    return jnp.concatenate([delta[2 * j : 2 * j + 1, :], delta[2 * j + 1 : 2 * j + 2, :]], 1)


def main_kernel(groups, listed, *refs):
    experts_ref = refs[0]
    near_b = refs[2]
    slots = refs[1:2] + refs[1 + groups : 2 + groups] + refs[3 : 1 + groups]
    (x_ref, ve_ref, se_ref, q_ref, q2t_ref, wk_ref, wv_ref) = refs[2 + groups : 9 + groups]
    (wout_ref, wup_ref, cot_ref, gact_ref) = refs[9 + groups : 13 + groups]
    wk_t, wv_t, wout_t, wup_t = refs[13 + groups : 17 + groups]
    outs = refs[17 + groups :]
    (send_a, send_b, keep, w_ref, inv_ref, gmixed_ref, delta_ref, kb_ref, vb_ref, ds_ref) = outs[:10]
    (act_ref, resid_ref, gres_ref), outs = outs[10:13], outs[13:]
    bits = groups.bit_length() - 1
    sends = outs[:bits]
    normed_s, mixed_s, gk_s, gv_s = outs[bits:]
    rows, width = x_ref.shape
    early = ve_ref.shape[0]
    place = lax.axis_index("blk")
    normed_s[:rows, :] = normalize(near_b[...].astype(f32))[0].astype(bf16)
    for e in range(listed):
        slot = experts_ref[:, e : e + 1] ^ place
        block = jnp.zeros((rows, width), f32)
        for i in range(groups):
            block = jnp.where(slot == i, slots[i][...].astype(f32), block)
        normed_s[(1 + e) * rows : (2 + e) * rows, :] = normalize(block)[0].astype(bf16)
    normed = normed_s[...]
    kb_ref[...] = dot(normed, wk_ref[...]).astype(bf16)
    vb_ref[...] = dot(normed, wv_ref[...]).astype(bf16)
    for j, cols in pair_columns():
        last = dot(kb_ref[:, cols], q2t_ref[j])
        first = se_ref[j]
        top = jnp.maximum(jnp.max(first, axis=0, keepdims=True), jnp.max(last, axis=0, keepdims=True))
        first = jnp.exp(first - top)
        last = jnp.exp(last - top)
        inv = 1.0 / (jnp.sum(first, axis=0, keepdims=True) + jnp.sum(last, axis=0, keepdims=True))
        w_ref[j, :early, :] = first
        w_ref[j, early:, :] = last
        inv_ref[j] = inv
        mixed = t_dot(ve_ref[:, cols], first.astype(bf16)) + t_dot(vb_ref[:, cols], last.astype(bf16))
        mixed_s[:, cols] = unhalve(mixed * inv).astype(bf16)

    mixed = mixed_s[...]
    resid = x_ref[...].astype(f32) + dot(mixed, wout_ref[...])
    resid_ref[...] = resid
    unit2, inv2 = normalize(resid)
    pre = dot(unit2.astype(bf16), wup_ref[...])
    square = pre * pre
    tanh = jnp.tanh(GELU_C * pre * (1.0 + GELU_A * square))
    act_ref[...] = (0.5 * pre * (1.0 + tanh)).astype(bf16)
    slope = 0.5 * (1.0 + tanh) + (0.5 * GELU_C) * pre * (1.0 - tanh * tanh) * (
        1.0 + (3.0 * GELU_A) * square
    )
    gpre = (gact_ref[...] * slope).astype(bf16)
    gres = cot_ref[...].astype(f32) + normalize_back(unit2, inv2, dot(gpre, wup_t[...]))
    gres_ref[...] = gres
    gmixed = dot(gres.astype(bf16), wout_t[...]).astype(bf16)
    gmixed_ref[...] = gmixed
    prod = gmixed.astype(f32) * mixed.astype(f32)
    high = prod.astype(bf16)
    low = (prod - high.astype(f32)).astype(bf16)
    head_of = lax.broadcasted_iota(jnp.int32, (H, width), 1) // HEAD
    ones = (head_of == lax.broadcasted_iota(jnp.int32, (H, width), 0)).astype(bf16)
    delta = dot_t(ones, high) + dot_t(ones, low)
    delta_ref[...] = delta

    for j, cols in pair_columns():
        ds_ref[j], gk_s[:, cols], gv_s[:, cols] = block_back(
            jnp.concatenate([ve_ref[rows:, cols], vb_ref[:, cols]], 0),
            q_ref[:, cols],
            gmixed[:, cols],
            w_ref[j, rows:, :],
            inv_ref[j],
            delta_row(delta, j),
        )
    parts = dot(gk_s[...], wk_t[...]) + dot(gv_s[...], wv_t[...])
    send_a[...] = parts[:rows].astype(bf16)
    send_b[...] = parts[rows : 2 * rows].astype(bf16)
    picked = [experts_ref[:, e : e + 1] ^ place for e in range(listed)]

    def far(slot):
        total = jnp.zeros((rows, width), f32)
        for e in range(listed):
            total = total + jnp.where(picked[e] == slot, parts[(2 + e) * rows : (3 + e) * rows], 0.0)
        return total

    keep[...] = far(0)
    for bit, slots_sent in enumerate(sent_slots(groups)):
        for i, slot in enumerate(slots_sent):
            sends[bit][i * rows : (i + 1) * rows, :] = far(slot).astype(bf16)


def rest_kernel(*refs):
    (w_ref, inv_ref, delta_ref, gmixed_ref, q_ref, ke_ref, ve_ref, kb_ref, ds_ref) = refs[:9]
    (keep_ref, act_ref, resid_ref, wq_ref, wk_ref, wv_ref, wdown_ref, out_ref, acc_ref) = refs[9:18]
    gq_s, gk_s, gv_s = refs[18:]
    rows = q_ref.shape[0]
    delta = delta_ref[...]
    for j, cols in pair_columns():
        ds, gk_s[:, cols], gv_s[:, cols] = block_back(
            ve_ref[:rows, cols],
            q_ref[:, cols],
            gmixed_ref[:, cols],
            w_ref[j, :rows, :],
            inv_ref[j],
            delta_row(delta, j),
        )
        total = t_dot(ke_ref[:rows, cols], ds) + t_dot(ke_ref[rows:, cols], ds_ref[j, :rows, :])
        total = total + t_dot(kb_ref[:, cols], ds_ref[j, rows:, :])
        gq_s[:, cols] = (unhalve(total) * SCALE).astype(bf16)
    acc_ref[...] = (
        keep_ref[...] + dot_t(gq_s[...], wq_ref[...]) + dot(gk_s[...], wk_ref[...]) + dot(gv_s[...], wv_ref[...])
    )
    out_ref[...] = (resid_ref[...] + dot(act_ref[...], wdown_ref[...])).astype(bf16)


def last_kernel(unit_ref, inv_ref, gres_ref, acc_ref, *refs):
    out_ref = refs[-1]
    rows = unit_ref.shape[0]
    total = acc_ref[...]
    for part in refs[:-1]:
        total = total + part[:rows, :].astype(f32)
    out_ref[...] = (gres_ref[...] + normalize_back(unit_ref[...], inv_ref[...], total)).astype(bf16)


def call(kernel, outs, args, scratch=(), flops=0, hbm=0):
    spaces = [pltpu.VMEM] * (len(args) - hbm) + [pltpu.HBM] * hbm
    return pl.pallas_call(
        kernel,
        out_shape=[jax.ShapeDtypeStruct(shape, dtype) for shape, dtype in outs],
        in_specs=[pl.BlockSpec(memory_space=space) for space in spaces],
        out_specs=[pl.BlockSpec(memory_space=pltpu.VMEM)] * len(outs),
        scratch_shapes=list(scratch),
        compiler_params=pltpu.CompilerParams(vmem_limit_bytes=40 * MIB),
        cost_estimate=pl.CostEstimate(flops=flops, bytes_accessed=4 * MIB, transcendentals=0),
    )(*args)


def on_device(nodes, experts_list, w_query, w_key, w_value, w_out, w_up, w_down, cotangent):
    rows, width = nodes.shape
    hidden = w_up.shape[1]
    groups = lax.axis_size("blk")
    domains = lax.axis_size("dom")
    listed = experts_list.shape[1]
    bits = groups.bit_length() - 1

    def exchanged(array, slot):
        return lax.ppermute(array, "blk", [(i, i ^ slot) for i in range(groups)])

    def across(array, bit):
        return exchanged(array, 1 << bit)

    pairs_a = [(i, i ^ 1) for i in range(domains)]
    pairs_b = []
    for i in range(1, domains, 2):
        pairs_b += [(i, (i + 1) % domains), ((i + 1) % domains, i)]

    near_a = lax.ppermute(nodes, "dom", pairs_a)
    near_b = lax.ppermute(nodes, "dom", pairs_b)
    held = {slot: exchanged(nodes, slot) for slot in range(2, groups)}

    def in_hbm(*arrays):
        return [pltpu.with_memory_space_constraint(array, pltpu.HBM) for array in arrays]

    given = [nodes, w_key, w_value, w_query, cotangent, w_up]
    x, w_key, w_value, w_query, cotangent, w_up, q, k, v, unit, inv_std = call(
        own_kernel,
        [(array.shape, array.dtype) for array in given]
        + [((rows, width), bf16)] * 3
        + [((rows, width), f32), ((rows, 1), f32)],
        in_hbm(*given),
        [pltpu.SemaphoreType.DMA((len(given),))],
        flops=6 * rows * width * width,
        hbm=len(given),
    )
    held[0] = x
    held[1] = exchanged(x, 1)
    early = 2 * rows
    late = (1 + listed) * rows
    keys = early + late
    ke, ve, se, gact, q2t, wk_t, wv_t, wout_t, wup_t = call(
        early_kernel,
        [((early, width), bf16)] * 2
        + [((H // 2, early, 2 * rows), f32), ((rows, hidden), f32), ((H // 2, PAIR, 2 * rows), bf16)]
        + [((width, width), bf16)] * 3
        + [((hidden, width), bf16)],
        [near_a, q, k, v, w_key, w_value, cotangent, w_down, w_out, w_up],
        flops=2 * early * width * (2 * width + 2 * rows),
    )
    sent = sent_slots(groups)
    send_a, send_b, keep, w, inv, gmixed, delta, kb, vb, ds, act, resid, gres, *sends = call(
        functools.partial(main_kernel, groups, listed),
        [((rows, width), bf16), ((rows, width), bf16), ((rows, width), f32)]
        + [((H // 2, keys, 2 * rows), f32), ((H // 2, 1, 2 * rows), f32)]
        + [((rows, width), bf16), ((H, rows), f32), ((late, width), bf16), ((late, width), bf16)]
        + [((H // 2, keys - rows, 2 * rows), bf16), ((rows, hidden), bf16)]
        + [((rows, width), f32)] * 2
        + [((len(slots) * rows, width), bf16) for slots in sent],
        [experts_list]
        + [x, near_b]
        + [held[slot] for slot in range(2, groups)]
        + [held[1]]
        + [x, ve, se, q, q2t, w_key, w_value]
        + [w_out, w_up, cotangent, gact, wk_t, wv_t, wout_t, wup_t],
        [pltpu.VMEM((late, width), bf16), pltpu.VMEM((rows, width), bf16)]
        + [pltpu.VMEM((keys - rows, width), bf16)] * 2,
        flops=2 * rows * width * (8 * keys + 4 * hidden),
    )
    from_a = lax.ppermute(send_a, "dom", pairs_a)
    received = [across(sends[0], 0)]
    from_b = lax.ppermute(send_b, "dom", pairs_b)
    for bit in range(1, bits):
        total = sends[bit].astype(f32)
        for lower, array in enumerate(received):
            blocks = array.reshape(-1, rows, width)[(1 << bit) >> (lower + 1) :: (2 << bit) >> (lower + 1)]
            total = total + blocks.reshape(-1, width).astype(f32)
        received.append(across(total.astype(bf16), bit))

    layer_out, acc = call(
        rest_kernel,
        [((rows, width), bf16), ((rows, width), f32)],
        [w, inv, delta, gmixed, q, ke, ve, kb, ds, keep, act, resid, w_query, wk_t, wv_t, w_down],
        [pltpu.VMEM((rows, width), bf16)] * 3,
        flops=2 * rows * width * (3 * width + hidden + 8 * rows),
    )
    (grad_nodes,) = call(
        last_kernel,
        [((rows, width), bf16)],
        [unit, inv_std, gres, acc, from_a, from_b] + received,
    )
    return (layer_out, grad_nodes)


def solution(mesh):
    split = P(("blk", "dom"), None)
    return jax.shard_map(
        on_device,
        mesh=mesh,
        in_specs=(split, split, P(), P(), P(), P(), P(), P(), split),
        out_specs=(split, split),
        check_vma=False,
    )
```

```python
import functools

import jax
import jax.numpy as jnp
from jax import lax
from jax.experimental import pallas as pl
from jax.experimental.pallas import tpu as pltpu
from jax.sharding import PartitionSpec as P

H = 8
HEAD = 64
EPS = 1e-05
SCALE = HEAD ** (-0.5)
PAIR = 2 * HEAD
GELU_C = 0.7978845608028654
GELU_A = 0.044715
MIB = 1 << 20

f32 = jnp.float32
bf16 = jnp.bfloat16


def dot(a, b):
    return jnp.dot(a, b, preferred_element_type=f32)


def dot_t(a, b):
    return lax.dot_general(a, b, (((1,), (1,)), ((), ())), preferred_element_type=f32)


def t_dot(a, b):
    return lax.dot_general(a, b, (((0,), (0,)), ((), ())), preferred_element_type=f32)


def normalize(values):
    mean_v = jnp.mean(values, axis=-1, keepdims=True)
    centered = values - mean_v
    inv_std = lax.rsqrt(jnp.mean(centered * centered, axis=-1, keepdims=True) + EPS)
    return (centered * inv_std, inv_std)


def normalize_back(unit, inv_std, upstream):
    return inv_std * (
        upstream
        - jnp.mean(upstream, axis=-1, keepdims=True)
        - unit * jnp.mean(upstream * unit, axis=-1, keepdims=True)
    )


def halves(rows):
    left = lax.broadcasted_iota(jnp.int32, rows.shape, 1) < HEAD
    zero = jnp.zeros_like(rows)
    return jnp.concatenate([jnp.where(left, rows, zero), jnp.where(left, zero, rows)], 0)


def halves_t(rows):
    turned = rows.T
    upper = lax.broadcasted_iota(jnp.int32, turned.shape, 0) < HEAD
    zero = jnp.zeros_like(turned)
    return jnp.concatenate([jnp.where(upper, turned, zero), jnp.where(upper, zero, turned)], 1)


def unhalve(both):
    n = both.shape[1] // 2
    first, second = both[:, :n], both[:, n:]
    upper = lax.broadcasted_iota(jnp.int32, first.shape, 0) < HEAD
    return jnp.where(upper, first, second).T


def sent_slots(groups):
    return [range(1 << bit, groups, 2 << bit) for bit in range(groups.bit_length() - 1)]


def fetch(given, held, sem):
    copies = [pltpu.make_async_copy(src, dst, sem.at[i]) for i, (src, dst) in enumerate(zip(given, held))]
    for copy in copies:
        copy.start()
    return copies


def own_kernel(*refs):
    given, held = refs[:6], refs[6:12]
    q_ref, k_ref, v_ref, unit_ref, inv_ref, sem = refs[12:]
    copies = fetch(given, held, sem)
    x_ref, wk_ref, wv_ref, wq_ref = held[:4]
    copies[0].wait()
    unit, inv = normalize(x_ref[...].astype(f32))
    unit_ref[...] = unit
    inv_ref[...] = inv
    normed = unit.astype(bf16)
    copies[1].wait()
    k_ref[...] = dot(normed, wk_ref[...]).astype(bf16)
    copies[2].wait()
    v_ref[...] = dot(normed, wv_ref[...]).astype(bf16)
    copies[3].wait()
    q_ref[...] = (dot(normed, wq_ref[...]) * SCALE).astype(bf16)
    copies[4].wait()
    copies[5].wait()


def pair_columns():
    return [(j, slice(j * PAIR, (j + 1) * PAIR)) for j in range(H // 2)]


def early_kernel(*refs):
    near_a, q_ref, k_ref, v_ref, wk_ref, wv_ref, cot_ref, wdown_ref, wout_ref, wup_ref = refs[:10]
    ke_ref, ve_ref, se_ref, gact_ref, q2t_ref, *turned = refs[10:]
    rows = q_ref.shape[0]
    unit, _ = normalize(near_a[...].astype(f32))
    normed = unit.astype(bf16)
    ke_ref[:rows, :] = k_ref[...]
    ve_ref[:rows, :] = v_ref[...]
    ke_ref[rows:, :] = dot(normed, wk_ref[...]).astype(bf16)
    ve_ref[rows:, :] = dot(normed, wv_ref[...]).astype(bf16)
    for j, cols in pair_columns():
        q2t = halves_t(q_ref[:, cols])
        q2t_ref[j] = q2t
        se_ref[j] = dot(ke_ref[:, cols], q2t)
    gact_ref[...] = dot_t(cot_ref[...], wdown_ref[...])
    for weight, out_ref in zip((wk_ref, wv_ref, wout_ref, wup_ref), turned):
        out_ref[...] = weight[...].T


def block_back(v, q, g, weights, inv, row):
    probs = weights * inv
    ds = (probs * (dot(v, halves_t(g)) - row)).astype(bf16)
    return ds, dot(ds, halves(q)).astype(bf16), dot(probs.astype(bf16), halves(g)).astype(bf16)


def delta_row(delta, j):
    return jnp.concatenate([delta[2 * j : 2 * j + 1, :], delta[2 * j + 1 : 2 * j + 2, :]], 1)


def main_kernel(groups, listed, *refs):
    experts_ref = refs[0]
    near_b = refs[2]
    slots = refs[1:2] + refs[1 + groups : 2 + groups] + refs[3 : 1 + groups]
    (x_ref, ve_ref, se_ref, q_ref, q2t_ref, wk_ref, wv_ref) = refs[2 + groups : 9 + groups]
    (wout_ref, wup_ref, cot_ref, gact_ref) = refs[9 + groups : 13 + groups]
    wk_t, wv_t, wout_t, wup_t = refs[13 + groups : 17 + groups]
    outs = refs[17 + groups :]
    (send_a, send_b, keep, w_ref, inv_ref, gmixed_ref, delta_ref, kb_ref, vb_ref, ds_ref) = outs[:10]
    (act_ref, resid_ref, gres_ref), outs = outs[10:13], outs[13:]
    bits = groups.bit_length() - 1
    sends = outs[:bits]
    normed_s, mixed_s, gk_s, gv_s = outs[bits:]
    rows, width = x_ref.shape
    early = ve_ref.shape[0]
    place = lax.axis_index("blk")
    normed_s[:rows, :] = normalize(near_b[...].astype(f32))[0].astype(bf16)
    for e in range(listed):
        slot = experts_ref[:, e : e + 1] ^ place
        block = jnp.zeros((rows, width), f32)
        for i in range(groups):
            block = jnp.where(slot == i, slots[i][...].astype(f32), block)
        normed_s[(1 + e) * rows : (2 + e) * rows, :] = normalize(block)[0].astype(bf16)
    normed = normed_s[...]
    kb_ref[...] = dot(normed, wk_ref[...]).astype(bf16)
    vb_ref[...] = dot(normed, wv_ref[...]).astype(bf16)
    for j, cols in pair_columns():
        last = dot(kb_ref[:, cols], q2t_ref[j])
        first = se_ref[j]
        top = jnp.maximum(jnp.max(first, axis=0, keepdims=True), jnp.max(last, axis=0, keepdims=True))
        first = jnp.exp(first - top)
        last = jnp.exp(last - top)
        inv = 1.0 / (jnp.sum(first, axis=0, keepdims=True) + jnp.sum(last, axis=0, keepdims=True))
        w_ref[j, :early, :] = first
        w_ref[j, early:, :] = last
        inv_ref[j] = inv
        mixed = t_dot(ve_ref[:, cols], first.astype(bf16)) + t_dot(vb_ref[:, cols], last.astype(bf16))
        mixed_s[:, cols] = unhalve(mixed * inv).astype(bf16)

    mixed = mixed_s[...]
    resid = x_ref[...].astype(f32) + dot(mixed, wout_ref[...])
    resid_ref[...] = resid
    unit2, inv2 = normalize(resid)
    pre = dot(unit2.astype(bf16), wup_ref[...])
    square = pre * pre
    tanh = jnp.tanh(GELU_C * pre * (1.0 + GELU_A * square))
    act_ref[...] = (0.5 * pre * (1.0 + tanh)).astype(bf16)
    slope = 0.5 * (1.0 + tanh) + (0.5 * GELU_C) * pre * (1.0 - tanh * tanh) * (
        1.0 + (3.0 * GELU_A) * square
    )
    gpre = (gact_ref[...] * slope).astype(bf16)
    gres = cot_ref[...].astype(f32) + normalize_back(unit2, inv2, dot(gpre, wup_t[...]))
    gres_ref[...] = gres
    gmixed = dot(gres.astype(bf16), wout_t[...]).astype(bf16)
    gmixed_ref[...] = gmixed
    prod = gmixed.astype(f32) * mixed.astype(f32)
    high = prod.astype(bf16)
    low = (prod - high.astype(f32)).astype(bf16)
    head_of = lax.broadcasted_iota(jnp.int32, (H, width), 1) // HEAD
    ones = (head_of == lax.broadcasted_iota(jnp.int32, (H, width), 0)).astype(bf16)
    delta = dot_t(jnp.concatenate([ones, ones], 1), jnp.concatenate([high, low], 1))
    delta_ref[...] = delta

    for j, cols in pair_columns():
        ds_ref[j], gk_s[:, cols], gv_s[:, cols] = block_back(
            jnp.concatenate([ve_ref[rows:, cols], vb_ref[:, cols]], 0),
            q_ref[:, cols],
            gmixed[:, cols],
            w_ref[j, rows:, :],
            inv_ref[j],
            delta_row(delta, j),
        )
    parts = dot(gk_s[...], wk_t[...]) + dot(gv_s[...], wv_t[...])
    send_a[...] = parts[:rows].astype(bf16)
    send_b[...] = parts[rows : 2 * rows].astype(bf16)
    picked = [experts_ref[:, e : e + 1] ^ place for e in range(listed)]

    def far(slot):
        total = 0.0
        for e in range(listed):
            total = total + jnp.where(picked[e] == slot, parts[(2 + e) * rows : (3 + e) * rows], 0.0)
        return total

    keep[...] = far(0)
    for bit, slots_sent in enumerate(sent_slots(groups)):
        for i, slot in enumerate(slots_sent):
            sends[bit][i * rows : (i + 1) * rows, :] = far(slot).astype(bf16)


def rest_kernel(*refs):
    (w_ref, inv_ref, delta_ref, gmixed_ref, q_ref, ke_ref, ve_ref, kb_ref, ds_ref) = refs[:9]
    (keep_ref, act_ref, resid_ref, wq_ref, wk_ref, wv_ref, wdown_ref, out_ref, acc_ref) = refs[9:18]
    gq_s, gk_s, gv_s = refs[18:]
    rows = q_ref.shape[0]
    delta = delta_ref[...]
    for j, cols in pair_columns():
        ds, gk_s[:, cols], gv_s[:, cols] = block_back(
            ve_ref[:rows, cols],
            q_ref[:, cols],
            gmixed_ref[:, cols],
            w_ref[j, :rows, :],
            inv_ref[j],
            delta_row(delta, j),
        )
        total = t_dot(ke_ref[:rows, cols], ds) + t_dot(ke_ref[rows:, cols], ds_ref[j, :rows, :])
        total = total + t_dot(kb_ref[:, cols], ds_ref[j, rows:, :])
        gq_s[:, cols] = (unhalve(total) * SCALE).astype(bf16)
    acc_ref[...] = (
        keep_ref[...] + dot_t(gq_s[...], wq_ref[...]) + dot(gk_s[...], wk_ref[...]) + dot(gv_s[...], wv_ref[...])
    )
    out_ref[...] = (resid_ref[...] + dot(act_ref[...], wdown_ref[...])).astype(bf16)


def last_kernel(unit_ref, inv_ref, gres_ref, acc_ref, *refs):
    out_ref = refs[-1]
    rows = unit_ref.shape[0]
    total = acc_ref[...]
    for part in refs[:-1]:
        total = total + part[:rows, :].astype(f32)
    out_ref[...] = (gres_ref[...] + normalize_back(unit_ref[...], inv_ref[...], total)).astype(bf16)


def call(kernel, outs, args, scratch=(), flops=0, hbm=0):
    spaces = [pltpu.VMEM] * (len(args) - hbm) + [pltpu.HBM] * hbm
    return pl.pallas_call(
        kernel,
        out_shape=[jax.ShapeDtypeStruct(shape, dtype) for shape, dtype in outs],
        in_specs=[pl.BlockSpec(memory_space=space) for space in spaces],
        out_specs=[pl.BlockSpec(memory_space=pltpu.VMEM)] * len(outs),
        scratch_shapes=list(scratch),
        compiler_params=pltpu.CompilerParams(vmem_limit_bytes=40 * MIB),
        cost_estimate=pl.CostEstimate(flops=flops, bytes_accessed=4 * MIB, transcendentals=0),
    )(*args)


def on_device(nodes, experts_list, w_query, w_key, w_value, w_out, w_up, w_down, cotangent):
    rows, width = nodes.shape
    hidden = w_up.shape[1]
    groups = lax.axis_size("blk")
    domains = lax.axis_size("dom")
    listed = experts_list.shape[1]
    bits = groups.bit_length() - 1

    def exchanged(array, slot):
        return lax.ppermute(array, "blk", [(i, i ^ slot) for i in range(groups)])

    def across(array, bit):
        return exchanged(array, 1 << bit)

    pairs_a = [(i, i ^ 1) for i in range(domains)]
    pairs_b = []
    for i in range(1, domains, 2):
        pairs_b += [(i, (i + 1) % domains), ((i + 1) % domains, i)]

    near_a = lax.ppermute(nodes, "dom", pairs_a)
    near_b = lax.ppermute(nodes, "dom", pairs_b)
    held = {slot: exchanged(nodes, slot) for slot in range(2, groups)}

    def in_hbm(*arrays):
        return [pltpu.with_memory_space_constraint(array, pltpu.HBM) for array in arrays]

    given = [nodes, w_key, w_value, w_query, cotangent, w_up]
    x, w_key, w_value, w_query, cotangent, w_up, q, k, v, unit, inv_std = call(
        own_kernel,
        [(array.shape, array.dtype) for array in given]
        + [((rows, width), bf16)] * 3
        + [((rows, width), f32), ((rows, 1), f32)],
        in_hbm(*given),
        [pltpu.SemaphoreType.DMA((len(given),))],
        flops=6 * rows * width * width,
        hbm=len(given),
    )
    held[0] = x
    held[1] = exchanged(x, 1)
    early = 2 * rows
    late = (1 + listed) * rows
    keys = early + late
    ke, ve, se, gact, q2t, wk_t, wv_t, wout_t, wup_t = call(
        early_kernel,
        [((early, width), bf16)] * 2
        + [((H // 2, early, 2 * rows), f32), ((rows, hidden), f32), ((H // 2, PAIR, 2 * rows), bf16)]
        + [((width, width), bf16)] * 3
        + [((hidden, width), bf16)],
        [near_a, q, k, v, w_key, w_value, cotangent, w_down, w_out, w_up],
        flops=2 * early * width * (2 * width + 2 * rows),
    )
    sent = sent_slots(groups)
    send_a, send_b, keep, w, inv, gmixed, delta, kb, vb, ds, act, resid, gres, *sends = call(
        functools.partial(main_kernel, groups, listed),
        [((rows, width), bf16), ((rows, width), bf16), ((rows, width), f32)]
        + [((H // 2, keys, 2 * rows), f32), ((H // 2, 1, 2 * rows), f32)]
        + [((rows, width), bf16), ((H, rows), f32), ((late, width), bf16), ((late, width), bf16)]
        + [((H // 2, keys - rows, 2 * rows), bf16), ((rows, hidden), bf16)]
        + [((rows, width), f32)] * 2
        + [((len(slots) * rows, width), bf16) for slots in sent],
        [experts_list]
        + [x, near_b]
        + [held[slot] for slot in range(2, groups)]
        + [held[1]]
        + [x, ve, se, q, q2t, w_key, w_value]
        + [w_out, w_up, cotangent, gact, wk_t, wv_t, wout_t, wup_t],
        [pltpu.VMEM((late, width), bf16), pltpu.VMEM((rows, width), bf16)]
        + [pltpu.VMEM((keys - rows, width), bf16)] * 2,
        flops=2 * rows * width * (8 * keys + 4 * hidden),
    )
    from_a = lax.ppermute(send_a, "dom", pairs_a)
    received = [across(sends[0], 0)]
    from_b = lax.ppermute(send_b, "dom", pairs_b)
    for bit in range(1, bits):
        total = sends[bit].astype(f32)
        for lower, array in enumerate(received):
            blocks = array.reshape(-1, rows, width)[(1 << bit) >> (lower + 1) :: (2 << bit) >> (lower + 1)]
            total = total + blocks.reshape(-1, width).astype(f32)
        received.append(across(total.astype(bf16), bit))

    layer_out, acc = call(
        rest_kernel,
        [((rows, width), bf16), ((rows, width), f32)],
        [w, inv, delta, gmixed, q, ke, ve, kb, ds, keep, act, resid, w_query, wk_t, wv_t, w_down],
        [pltpu.VMEM((rows, width), bf16)] * 3,
        flops=2 * rows * width * (3 * width + hidden + 8 * rows),
    )
    (grad_nodes,) = call(
        last_kernel,
        [((rows, width), bf16)],
        [unit, inv_std, gres, acc, from_a, from_b] + received,
    )
    return (layer_out, grad_nodes)


def solution(mesh):
    split = P(("blk", "dom"), None)
    return jax.shard_map(
        on_device,
        mesh=mesh,
        in_specs=(split, split, P(), P(), P(), P(), P(), P(), split),
        out_specs=(split, split),
        check_vma=False,
    )
```
